32 devices in a mesh: gx: 4 (over x, core), gy: 2 (over y), gz: 4 (over z).
Axes of the slice: x: 2, y: 2, z: 4, core: 2. Of those that a mesh axis runs over, the one named last changes fastest.
Arguments:
- energy: float32 [24, 24, 768], P('gx', 'gy', 'gz'), may hold values from 0.5 to 18, as said below
- density: float32 [8, 8, 256], P('gx', 'gy', 'gz'), may hold values from 0.125 to 1
- region: int32 [8, 8, 256], P('gx', 'gy', 'gz'), may hold values from 0 to 2
- gamma_table: float32 [3], replicated, may hold values from 1.3 to 1.9
Outputs:
- acceleration: float32 [3, 16, 16, 512], P(None, 'gx', 'gy', 'gz')
- residual: float32 [3, 16, 16, 512], P(None, 'gx', 'gy', 'gz')
The draws below stay inside these ranges and needn't reach their ends.
Inputs may be any that keep to these rules, and one draw needn't show every extreme that they name: energy is positive.
All inputs are finite; a program needn't handle non-finite values.
Results may differ from the reference program's by a relative error of at most 0.0001.
Values sent between devices are 32-bit elements; how exact they have to be, the bound alone decides.
A program may use at most 64 MiB of HBM per device.

```python
import math
import jax
import jax.numpy as jnp
from jax import lax

ITERS = 2
MATERIAL_ZONES = 3
ELEMENTS_X = 8
ELEMENTS_Y = 8
ELEMENTS_Z = 256


def draw_energy(key, part):
    shape_values = (3 * ELEMENTS_X, 3 * ELEMENTS_Y, 3 * ELEMENTS_Z)
    first = jax.random.fold_in(jax.random.fold_in(key, 17), 0)
    along_x = 1.0 + 2.0 * jnp.arange(3 * ELEMENTS_X, dtype=jnp.float32) / (3 * ELEMENTS_X - 1)
    logs = jax.random.uniform(first, shape_values, jnp.float32, jnp.log(0.5), jnp.log(2.0))
    outcome_field = jnp.exp(logs) * along_x[:, None, None]
    return outcome_field.astype(jnp.float32)


def touch_ends(entries, own_key, least, top_value):
    extent = entries.shape
    place = [jax.random.randint(jax.random.fold_in(own_key, axis), (), 0, extent[axis]) for axis in range(len(extent))]
    entries = entries.at[tuple(place)].set(least)
    longest = extent.index(max(extent))
    place[longest] = (place[longest] + 1) % extent[longest]
    return entries.at[tuple(place)].set(top_value)


def steps_of(key, extent, shards, low, top_value):
    gain = 1.0
    for position, blocks in shards:
        steps = jax.random.uniform(jax.random.fold_in(jax.random.fold_in(key, 6), position), (blocks,), jnp.float32, low / len(shards), top_value / len(shards))
        gain = gain * jnp.repeat(jnp.exp(steps), extent[position] // blocks).reshape((-1,) + (1,) * (len(extent) - 1 - position))
    return gain


def setup_inputs(seed: int = 0) -> dict:
    key_list = jax.random.split(jax.random.key(seed), 5)
    energy = draw_energy(jax.random.fold_in(key_list[4], 71), 0)
    density = jnp.clip(jnp.exp(math.log(1.0) - 2.0794415 * jax.random.uniform(key_list[1], (ELEMENTS_X, ELEMENTS_Y, ELEMENTS_Z), jnp.float32) ** steps_of(key_list[1], (ELEMENTS_X, ELEMENTS_Y, ELEMENTS_Z), ((0, 4), (1, 2), (2, 4)), -0.2, 0.2)), 0.125, 1.0)
    region = touch_ends(jax.random.randint(key_list[2], (ELEMENTS_X, ELEMENTS_Y, ELEMENTS_Z), 0, MATERIAL_ZONES), jax.random.fold_in(key_list[2], 1), 0, MATERIAL_ZONES - 1).astype(jnp.int32)
    gamma_table = jnp.clip(jax.random.uniform(key_list[3], (MATERIAL_ZONES,), jnp.float32, 1.3, 1.9), 1.3, 1.9)
    return {"energy": energy, "density": density, "region": region, "gamma_table": gamma_table}


WEIGHTS = [5.0 / 18.0, 8.0 / 18.0, 5.0 / 18.0]

def line_tables():
    root = math.sqrt(0.15)
    spots = [0.5 - root, 0.5, 0.5 + root]
    values = [[2.0 * (spot - 0.5) * (spot - 1.0), -4.0 * spot * (spot - 1.0), 2.0 * spot * (spot - 0.5)] for spot in spots]
    slopes = [[4.0 * spot - 3.0, -8.0 * spot + 4.0, 4.0 * spot - 1.0] for spot in spots]
    return (values, slopes)

def to_points(field, axis, table):
    count = (field.shape[axis] - 1) // 2
    parts = [lax.slice_in_dim(field, offset, offset + 2 * count - 1, 2, axis) for offset in range(3)]
    rows = [table[member][0] * parts[0] + table[member][1] * parts[1] + table[member][2] * parts[2] for member in range(3)]
    joined = jnp.stack(rows, axis=axis + 1)
    shape_values = list(field.shape)
    shape_values[axis] = 3 * count
    return joined.reshape(shape_values)

def to_nodes(points, axis, table):
    count = points.shape[axis] // 3
    shape_values = list(points.shape)
    grouped = points.reshape(shape_values[:axis] + [count, 3] + shape_values[axis + 1:])
    parts = [lax.index_in_dim(grouped, member, axis + 1, keepdims=False) for member in range(3)]
    terms = [table[0][offset] * parts[0] + table[1][offset] * parts[1] + table[2][offset] * parts[2] for offset in range(3)]
    widths_end = [(0, 0)] * len(shape_values)
    widths_end[axis] = (0, 1)
    widths_front = [(0, 0)] * len(shape_values)
    widths_front[axis] = (1, 0)
    evens = jnp.pad(terms[0], widths_end) + jnp.pad(terms[2], widths_front)
    woven = jnp.stack([lax.slice_in_dim(evens, 0, count, 1, axis), terms[1]], axis=axis + 1)
    shape_two = list(terms[1].shape)
    shape_two[axis] = 2 * count
    woven = woven.reshape(shape_two)
    return jnp.concatenate([woven, lax.slice_in_dim(evens, count, count + 1, 1, axis)], axis=axis)

def mass_apply(nodes, coef):
    values, slopes = line_tables()
    points = to_points(to_points(to_points(nodes, 0, values), 1, values), 2, values)
    points = points * coef
    return to_nodes(to_nodes(to_nodes(points, 2, values), 1, values), 0, values)

def force_contributions(pressure_weighted):
    values, slopes = line_tables()
    force_x = to_nodes(to_nodes(to_nodes(pressure_weighted, 0, slopes), 1, values), 2, values)
    force_y = to_nodes(to_nodes(to_nodes(pressure_weighted, 0, values), 1, slopes), 2, values)
    force_z = to_nodes(to_nodes(to_nodes(pressure_weighted, 0, values), 1, values), 2, slopes)
    return jnp.stack([force_x, force_y, force_z])

def expand(values):
    return jnp.repeat(jnp.repeat(jnp.repeat(values, 3, 0), 3, 1), 3, 2)

def lookup(region, gamma_table):
    gamma_elem = jnp.zeros(region.shape, gamma_table.dtype)
    for index in range(MATERIAL_ZONES):
        gamma_elem = gamma_elem + jnp.where(region == index, gamma_table[index], 0.0)
    return gamma_elem

def reference(energy, density, region, gamma_table):
    line_entries = jnp.array(WEIGHTS, energy.dtype)
    quadrature_weights = jnp.tile(line_entries, ELEMENTS_X)[:, None, None] * jnp.tile(line_entries, ELEMENTS_Y)[None, :, None] * jnp.tile(line_entries, ELEMENTS_Z)[None, None, :]
    gamma_elem = lookup(region, gamma_table)
    pressure_weighted = expand((gamma_elem - 1.0) * density) * energy * quadrature_weights
    coef = expand(density) * quadrature_weights
    mask_x = (jnp.arange(2 * ELEMENTS_X) != 0).astype(energy.dtype)
    mask_y = (jnp.arange(2 * ELEMENTS_Y) != 0).astype(energy.dtype)
    depth_mask = (jnp.arange(2 * ELEMENTS_Z) != 0).astype(energy.dtype)
    boundary_mask = (mask_x[:, None, None] * mask_y[None, :, None] * depth_mask[None, None, :])[None]
    corner_force = force_contributions(pressure_weighted)[:, :2 * ELEMENTS_X, :2 * ELEMENTS_Y, :2 * ELEMENTS_Z] * boundary_mask

    def operate(field):
        padded = jnp.pad(field, ((0, 0), (0, 1), (0, 1), (0, 1)))

        def single(nodes):
            return mass_apply(nodes, coef)
        outcome_field = lax.map(single, padded)
        return outcome_field[:, :2 * ELEMENTS_X, :2 * ELEMENTS_Y, :2 * ELEMENTS_Z] * boundary_mask
    solution = jnp.zeros_like(corner_force)
    residual = corner_force
    direction = corner_force
    norm_now = lax.optimization_barrier(jnp.sum(residual * residual, axis=(1, 2, 3)))
    for step in range(ITERS):
        image = operate(direction)
        alpha = norm_now / lax.optimization_barrier(jnp.sum(direction * image, axis=(1, 2, 3)))
        solution = solution + alpha[:, None, None, None] * direction
        residual = residual - alpha[:, None, None, None] * image
        norm_next = lax.optimization_barrier(jnp.sum(residual * residual, axis=(1, 2, 3)))
        direction = residual + (norm_next / norm_now)[:, None, None, None] * direction
        norm_now = norm_next
    return (solution, residual)
```

```python
import functools
import math

import jax
import jax.numpy as jnp
import numpy as np
from jax import lax
from jax.experimental import pallas as pl
from jax.experimental.pallas import tpu as pltpu
from jax.sharding import PartitionSpec as P

MESH = pl.DeviceIdType.MESH
AXES = ("gx", "gy", "gz")
WEIGHTS = [5.0 / 18.0, 8.0 / 18.0, 5.0 / 18.0]
SUB = 8
PHASES = 3


def line_tables():
    root = math.sqrt(0.15)
    spots = [0.5 - root, 0.5, 0.5 + root]
    values = [
        [2.0 * (spot - 0.5) * (spot - 1.0), -4.0 * spot * (spot - 1.0), 2.0 * spot * (spot - 0.5)]
        for spot in spots
    ]
    slopes = [[4.0 * spot - 3.0, -8.0 * spot + 4.0, 4.0 * spot - 1.0] for spot in spots]
    return np.array(values), np.array(slopes)


def line_mass():
    values, _ = line_tables()
    return values.T @ np.diag(WEIGHTS) @ values


def z_matrix(cz, lanes):
    values, slopes = line_tables()
    out = np.zeros((3 * cz, 6, lanes), np.float32)
    for k in range(3):
        for a in range(3):
            for e in range(cz):
                out[3 * e + a, k, e] = WEIGHTS[a] * values[a][k]
                out[3 * e + a, 3 + k, e] = WEIGHTS[a] * slopes[a][k]
    return out.reshape(3 * cz, 6 * lanes)


def line_matrix(count, table):
    out = np.zeros((2 * count + 1, 3 * count))
    for i in range(count):
        for a in range(3):
            for k in range(3):
                out[2 * i + k, 3 * i + a] += WEIGHTS[a] * table[a][k]
    return out


def plane_matrix(cx, cy):
    values, slopes = line_tables()
    vx, sx = line_matrix(cx, values), line_matrix(cx, slopes)
    vy, sy = line_matrix(cy, values), line_matrix(cy, slopes)
    nx, ny, points = 2 * cx + 1, 2 * cy + 1, 9 * cx * cy
    out = np.zeros((ny, nx, SUB, 2, points), np.float32)
    for c, (mx, my, part) in enumerate(((sx, vy, 0), (vx, sy, 0), (vx, vy, 1))):
        block = np.einsum("xp,yq->yxpq", mx, my).reshape(ny, nx, points)
        out[:, :, c, part] = block
        out[:, :, c + 4, part] = block
    return out.reshape(ny * nx * SUB, 2 * points)


def weave_matrix(cz, lanes):
    out = np.zeros((2, lanes, 2 * cz), np.float32)
    for e in range(cz):
        out[0, e, 2 * e] = 1.0
        out[1, e, 2 * e + 1] = 1.0
    return out.reshape(2 * lanes, 2 * cz)


def exact_dot(a, b):
    return jnp.dot(a, b, precision=lax.Precision.HIGHEST, preferred_element_type=jnp.float32)


def reduction_stages(sizes):
    if math.prod(sizes) <= 64:
        return [(0, 1, 2)]
    return [(0,), (1,), (2,)]


def group_size(stage, sizes):
    return math.prod(sizes[axis] for axis in stage)


def axis_directions(index, size):
    if size == 1:
        return []
    if size == 2:
        return [(0, 0, 1 - 2 * index, None)]
    return [(0, 1, -1, index > 0), (1, 0, 1, index < size - 1)]


def pick(step, low, high):
    if isinstance(step, int):
        return low if step < 0 else high
    return jnp.where(step > 0, high, low)


def under(conditions, action):
    conditions = [c for c in conditions if c is not None]
    if not conditions:
        action()
        return
    both = conditions[0]
    for c in conditions[1:]:
        both = jnp.logical_and(both, c)
    pl.when(both)(action)


def kernel(
    sizes, cx, cy, cz, lanes,
    energy, density, region, gamma, z_mat, plane_mat, weave_mat,
    acc_out, res_out,
    points, fac, fac_points, dens, part, full, rows, z_part, x_buf, y_buf, xy_buf, z_buf,
    send_sem, recv_sem, *stage_refs,
):
    nx, ny = 2 * cx + 1, 2 * cy + 1
    nodes = nx * ny
    place = [lax.axis_index(name) for name in AXES]
    stages = reduction_stages(sizes)
    centre = (2, 2, 0, None)
    dirs = [axis_directions(place[axis], sizes[axis]) for axis in range(3)]
    sides = [d + [centre] for d in dirs]

    def target(step_x, step_y, step_z):
        return (place[0] + step_x, place[1] + step_y, place[2] + step_z)

    def partner(stage, offset):
        mine = 0
        for axis in stage:
            mine = mine * sizes[axis] + place[axis]
        other = lax.rem(mine + offset, group_size(stage, sizes))
        where = list(place)
        for axis in reversed(stage):
            where[axis] = lax.rem(other, sizes[axis])
            other = lax.div(other, sizes[axis])
        return tuple(where), mine

    for ref in (x_buf, y_buf, xy_buf, z_buf):
        ref[...] = jnp.zeros_like(ref)

    barrier = pltpu.get_barrier_semaphore()
    for stage in stages:
        size = group_size(stage, sizes)

        @pl.loop(1, size)
        def _(offset, stage=stage):
            where, _mine = partner(stage, offset)
            pl.semaphore_signal(barrier, inc=1, device_id=where, device_id_type=MESH)

    for xp in range(3 * cx):
        points[pl.ds(xp * 3 * cy, 3 * cy), :] = energy[xp]
    gamma_elem = jnp.zeros(region.shape, jnp.float32)
    for index in range(gamma.shape[0]):
        gamma_elem = gamma_elem + jnp.where(region[...] == index, gamma[index], 0.0)
    factor = (gamma_elem - 1.0) * density[...]
    fac[...] = jnp.zeros_like(fac)
    dens[...] = jnp.zeros_like(dens)
    for i in range(cx):
        fac[pl.ds(i * cy, cy), pl.ds(0, cz)] = factor[i]
        dens[pl.ds(i * cy, cy), pl.ds(0, cz)] = density[i]
    for xp in range(3 * cx):
        for k in range(cy):
            row = fac[pl.ds((xp // 3) * cy + k, 1), :]
            fac_points[pl.ds(xp * 3 * cy + 3 * k, 3), :] = jnp.broadcast_to(row, (3, lanes))
    sums = exact_dot(points[...], z_mat[...])
    scaled = [sums[:, k * lanes : (k + 1) * lanes] * fac_points[...] for k in range(6)]
    even = jnp.concatenate(
        [scaled[0] + pltpu.roll(scaled[2], 1, 1), scaled[3] + pltpu.roll(scaled[5], 1, 1)], axis=0
    )
    odd = jnp.concatenate([scaled[1], scaled[4]], axis=0)
    force = exact_dot(plane_mat[...], jnp.concatenate([even, odd], axis=1))
    sub = lax.broadcasted_iota(jnp.int32, (1, SUB, lanes), 1)
    lane = lax.broadcasted_iota(jnp.int32, (1, SUB, lanes), 2)
    is_even = sub < 4
    e_part = force[:, :lanes].reshape(nodes, SUB, lanes)
    o_part = force[:, lanes:].reshape(nodes, SUB, lanes)
    part[0] = jnp.where(is_even, e_part, o_part).reshape(ny, nx, SUB, lanes)

    used = jnp.logical_and(lax.rem(sub, 4) < 3, lane < jnp.where(is_even, cz + 1, cz))
    wall_low = jnp.logical_and(place[2] == 0, jnp.logical_and(is_even, lane == 0))
    wall_high = jnp.logical_and(
        place[2] == sizes[2] - 1, jnp.logical_and(is_even, lane == cz)
    )
    keep = jnp.where(
        jnp.logical_and(used, jnp.logical_not(jnp.logical_or(wall_low, wall_high))), 1.0, 0.0
    )
    owned = jnp.where(lane < cz, 1.0, 0.0)
    ends = [jnp.logical_and(is_even, lane == 0), jnp.logical_and(is_even, lane == cz)]
    spot = lax.broadcasted_iota(jnp.int32, (nodes, SUB, 128), 0)
    pack_lane = lax.broadcasted_iota(jnp.int32, (nodes, SUB, 128), 2)
    pack_hot = jnp.where(spot == pack_lane, 1.0, 0.0)
    flat_lane = lax.broadcasted_iota(jnp.int32, (SUB, 128), 1)
    lane_x, lane_y = lax.rem(flat_lane, nx), lax.div(flat_lane, nx)

    def copies(phase, side_x, side_y, side_z):
        (sx, tx, dx, _), (sy, ty, dy, _), (sz, tz, dz, _) = side_x, side_y, side_z
        here, there = [phase * 27 + (a * 3 + b) * 3 + c for a, b, c in ((sx, sy, sz), (tx, ty, tz))]
        xf, yf = pick(dx, 0, nx - 1), pick(dy, 0, ny - 1)
        if sz != 2:
            src = z_part.at[phase, pick(dz, 0, 1)]
            dst, own = z_buf.at[phase, tz, tx, ty], z_buf.at[phase, sz, sx, sy]
        elif sy == 2:
            src = part.at[phase, :, xf]
            dst, own = x_buf.at[phase, tx], x_buf.at[phase, sx]
        elif sx == 2:
            src = part.at[phase, yf]
            dst, own = y_buf.at[phase, ty], y_buf.at[phase, sy]
        else:
            src = part.at[phase, yf, xf]
            dst, own = xy_buf.at[phase, tx, ty], xy_buf.at[phase, sx, sy]

        def make(dst_ref, slot):
            return pltpu.make_async_remote_copy(
                src_ref=src, dst_ref=dst_ref, send_sem=send_sem.at[here], recv_sem=recv_sem.at[slot],
                device_id=target(dx, dy, dz), device_id_type=MESH,
            )

        return lambda: make(dst, there), lambda: make(own, here)

    def each(phase, plane, action):
        groups = {}
        for side_z in [centre] if plane else dirs[2]:
            for side_x in sides[0]:
                for side_y in sides[1]:
                    if side_z[0] == 2 and side_x[0] == 2 and side_y[0] == 2:
                        continue
                    conditions = (side_x[3], side_y[3], side_z[3])
                    key = tuple(None if c is None else s[0] for c, s in zip(conditions, (side_x, side_y, side_z)))
                    groups.setdefault(key, (conditions, []))[1].append((side_x, side_y, side_z))
        for conditions, members in groups.values():

            def run(members=members):
                for member in members:
                    action(copies(phase, *member))

            under(conditions, run)

    def start(phase):
        each(phase, True, lambda pair: pair[0]().start())
        whole = part[phase].reshape(nodes, SUB, lanes)
        for side, at in ((0, 0), (1, cz)):
            z_part[phase, side] = jnp.sum(whole[:, :, at : at + 1] * pack_hot, axis=0)
        each(phase, False, lambda pair: pair[0]().start())

    def finish(phase):
        each(phase, True, lambda pair: pair[1]().wait_recv())
        full[phase] = part[phase]
        for sx, _, dx, _ in dirs[0]:
            xf = pick(dx, 0, nx - 1)
            full[phase, :, xf] = full[phase, :, xf] + x_buf[phase, sx]
        for sy, _, dy, _ in dirs[1]:
            yf = pick(dy, 0, ny - 1)
            full[phase, yf] = full[phase, yf] + y_buf[phase, sy]
            for sx, _, dx, _ in dirs[0]:
                xf = pick(dx, 0, nx - 1)
                full[phase, yf, xf] = full[phase, yf, xf] + xy_buf[phase, sx, sy]
        each(phase, False, lambda pair: pair[1]().wait_recv())
        whole = full[phase].reshape(nodes, SUB, lanes)
        for sz, _, dz, _ in dirs[2]:
            tile = z_buf[phase, sz, 2, 2]
            for sx, _, dx, _ in sides[0]:
                for sy, _, dy, _ in sides[1]:
                    if sx == 2 and sy == 2:
                        continue
                    moved = pltpu.roll(
                        z_buf[phase, sz, sx, sy],
                        lax.rem(dx * (nx - 1) + dy * (ny - 1) * nx + 128, 128), 1,
                    )
                    good = flat_lane < nodes
                    if sx != 2:
                        good = jnp.logical_and(good, lane_x == pick(dx, 0, nx - 1))
                    if sy != 2:
                        good = jnp.logical_and(good, lane_y == pick(dy, 0, ny - 1))
                    tile = tile + jnp.where(good, moved, 0.0)
            spread = jnp.sum(tile[None] * pack_hot, axis=2, keepdims=True)
            end = pick(dz, ends[0], ends[1])
            whole = whole + jnp.where(end, spread, 0.0)
        full[phase] = (whole * keep).reshape(ny, nx, SUB, lanes)
        for axis, last in ((0, nx - 1), (1, ny - 1)):
            for at, here in ((0, place[axis] == 0), (last, place[axis] == sizes[axis] - 1)):

                @pl.when(here)
                def _(axis=axis, at=at):
                    if axis == 0:
                        full[phase, :, at] = jnp.zeros((ny, SUB, lanes), jnp.float32)
                    else:
                        full[phase, at] = jnp.zeros((nx, SUB, lanes), jnp.float32)

    mass = [[float(v) for v in line] for line in line_mass()]

    def combine(weights, parts):
        return weights[0] * parts[0] + weights[1] * parts[1] + weights[2] * parts[2]

    on_even, on_odd, on_next = [
        jnp.where(is_even, mass[0][k], mass[1][k]).astype(jnp.float32) for k in range(3)
    ]
    even_only = jnp.where(is_even, 1.0, 0.0)

    def apply_mass(source, phase):
        lines = [full[source, y] for y in range(ny)]
        along_y = jnp.concatenate(
            [combine(mass[l], lines[2 * k : 2 * k + 3])[None] for k in range(cy) for l in range(3)],
            axis=0,
        )
        at_x = [along_y[:, x] for x in range(nx)]
        blocks = []
        for i in range(cx):
            tiles = [
                jnp.broadcast_to(dens[pl.ds(i * cy + k, 1), :], (SUB, lanes))[None]
                for k in range(cy)
                for _ in range(3)
            ]
            rho = jnp.concatenate(tiles, axis=0)
            rho_next = rho * even_only
            for j in range(3):
                t = combine(mass[j], at_x[2 * i : 2 * i + 3])
                other = pltpu.roll(t, 4, 1)
                evens, odds = jnp.where(is_even, t, other), jnp.where(is_even, other, t)
                following = pltpu.roll(evens, lanes - 1, 2)
                own = on_even * evens + on_odd * odds + on_next * following
                far = combine(mass[2], (evens, odds, following))
                blocks.append(rho * own + pltpu.roll(rho_next * far, 1, 2))
        for x in range(nx):
            i, odd_x = divmod(x, 2)
            if odd_x:
                column = blocks[3 * i + 1]
            elif x == 0:
                column = blocks[0]
            elif x == nx - 1:
                column = blocks[3 * i - 1]
            else:
                column = blocks[3 * i] + blocks[3 * i - 1]
            for y in range(ny):
                k, odd_y = divmod(y, 2)
                if odd_y:
                    value = column[3 * k + 1]
                elif y == 0:
                    value = column[0]
                elif y == ny - 1:
                    value = column[3 * k - 1]
                else:
                    value = column[3 * k] + column[3 * k - 1]
                part[phase, y, x] = value

    def woven(phase):
        rows[...] = full[phase].reshape(nodes * SUB, lanes)
        halves = []
        for first in (0, 4):
            halves.append(jnp.concatenate(
                [
                    rows[pl.ds(x * SUB + first + c, 2 * cy, stride=nx * SUB), :]
                    for c in range(3)
                    for x in range(2 * cx)
                ],
                axis=0,
            ))
        return exact_dot(jnp.concatenate(halves, axis=1), weave_mat[...])

    if sum(group_size(stage, sizes) - 1 for stage in stages):
        pl.semaphore_wait(barrier, sum(group_size(stage, sizes) - 1 for stage in stages))
    start(0)
    finish(0)
    apply_mass(0, 1)
    start(1)
    finish(1)
    apply_mass(1, 2)
    start(2)

    force_own = full[0, : ny - 1, : nx - 1].reshape(4 * cx * cy, SUB, lanes) * owned
    image_own = full[1, : ny - 1, : nx - 1].reshape(4 * cx * cy, SUB, lanes) * owned
    products = [
        jnp.sum(force_own * force_own, axis=0),
        jnp.sum(force_own * image_own, axis=0),
        jnp.sum(image_own * image_own, axis=0),
        jnp.sum((full[1] * part[2]).reshape(nodes, SUB, lanes), axis=0),
    ]
    flat_sub = lax.broadcasted_iota(jnp.int32, (SUB, 128), 0)
    message = jnp.zeros((SUB, 128), jnp.float32)
    for k, product in enumerate(products):
        hot = flat_lane == 4 * lax.rem(flat_sub, 4) + k
        message = message + jnp.where(hot, jnp.sum(product, axis=1, keepdims=True), 0.0)
    total = jnp.sum(message, axis=0, keepdims=True)

    woven_force, woven_image = None, None
    for number, stage in enumerate(stages):
        slots, stage_send, stage_recv = stage_refs[3 * number : 3 * number + 3]
        size = group_size(stage, sizes)
        if size == 1:
            continue
        _, mine = partner(stage, 0)
        slots[mine] = total

        @pl.loop(1, size)
        def _(offset, stage=stage, slots=slots, stage_send=stage_send, stage_recv=stage_recv):
            where, at = partner(stage, offset)
            pltpu.make_async_remote_copy(
                src_ref=slots.at[at], dst_ref=slots.at[at],
                send_sem=stage_send, recv_sem=stage_recv,
                device_id=where, device_id_type=MESH,
            ).start()

        if number == 0:
            woven_force, woven_image = woven(0), woven(1)
            finish(2)
        where, _ = partner(stage, 1)
        others = slots.at[pl.ds(0, size - 1)]
        wait = pltpu.make_async_remote_copy(
            src_ref=others, dst_ref=others, send_sem=stage_send, recv_sem=stage_recv,
            device_id=where, device_id_type=MESH,
        )
        wait.wait_recv()
        wait.wait_send()
        total = jnp.sum(slots[...], axis=0)
    if woven_force is None:
        woven_force, woven_image = woven(0), woven(1)
        finish(2)
    woven_second = woven(2)

    row_lane = lax.broadcasted_iota(jnp.int32, (1, 128), 1)
    live = jnp.logical_and(lax.rem(row_lane, 4) == 0, row_lane < 12)
    ff, fi, ii, si = [
        jnp.where(live, total if k == 0 else pltpu.roll(total, 128 - k, 1), 1.0) for k in range(4)
    ]
    alpha = ff / fi
    next_norm = alpha * alpha * ii - ff
    ratio = next_norm / ff
    curvature = fi - 2.0 * alpha * ii + alpha * alpha * si - ratio * next_norm / alpha
    second = next_norm / curvature
    outer = alpha + second * (1.0 + ratio)
    inner = alpha * second
    per = 2 * cx * 2 * cy
    for c in range(3):
        hot = row_lane == 4 * c
        a = jnp.sum(jnp.where(hot, outer, 0.0), axis=1, keepdims=True)
        b = jnp.sum(jnp.where(hot, inner, 0.0), axis=1, keepdims=True)
        here = slice(c * per, (c + 1) * per)
        f, q, s = woven_force[here], woven_image[here], woven_second[here]
        acc_out[c] = (a * f - b * q).reshape(2 * cx, 2 * cy, 2 * cz)
        res_out[c] = (f - a * q + b * s).reshape(2 * cx, 2 * cy, 2 * cz)

    for phase in range(PHASES):
        each(phase, True, lambda pair: pair[0]().wait_send())
        each(phase, False, lambda pair: pair[0]().wait_send())


def solution(mesh):
    sizes = tuple(mesh.shape[name] for name in AXES)

    def on_device(energy, density, region, gamma_table):
        cx, cy, cz = density.shape
        lanes = -(-(cz + 1) // 128) * 128
        nx, ny = 2 * cx + 1, 2 * cy + 1
        out = jax.ShapeDtypeStruct((3, 2 * cx, 2 * cy, 2 * cz), jnp.float32)
        vmem = pl.BlockSpec(memory_space=pltpu.VMEM)
        tile = (SUB, lanes)
        scratch = [
            pltpu.VMEM((9 * cx * cy, 3 * cz), jnp.float32),
            pltpu.VMEM((cx * cy, lanes), jnp.float32),
            pltpu.VMEM((9 * cx * cy, lanes), jnp.float32),
            pltpu.VMEM((cx * cy, lanes), jnp.float32),
            pltpu.VMEM((PHASES, ny, nx) + tile, jnp.float32),
            pltpu.VMEM((PHASES, ny, nx) + tile, jnp.float32),
            pltpu.VMEM((ny * nx * SUB, lanes), jnp.float32),
            pltpu.VMEM((PHASES, 2, SUB, 128), jnp.float32),
            pltpu.VMEM((PHASES, 2, ny) + tile, jnp.float32),
            pltpu.VMEM((PHASES, 2, nx) + tile, jnp.float32),
            pltpu.VMEM((PHASES, 2, 2) + tile, jnp.float32),
            pltpu.VMEM((PHASES, 2, 3, 3, SUB, 128), jnp.float32),
            pltpu.SemaphoreType.DMA((PHASES * 27,)),
            pltpu.SemaphoreType.DMA((PHASES * 27,)),
        ]
        for stage in reduction_stages(sizes):
            scratch += [
                pltpu.VMEM((group_size(stage, sizes), 1, 128), jnp.float32),
                pltpu.SemaphoreType.DMA,
                pltpu.SemaphoreType.DMA,
            ]
        return pl.pallas_call(
            functools.partial(kernel, sizes, cx, cy, cz, lanes),
            out_shape=(out, out),
            in_specs=[vmem] * 3 + [pl.BlockSpec(memory_space=pltpu.SMEM)] + [vmem] * 3,
            out_specs=(vmem, vmem),
            scratch_shapes=scratch,
            compiler_params=pltpu.CompilerParams(
                collective_id=0, has_side_effects=True, vmem_limit_bytes=32 * 1024 * 1024
            ),
        )(
            energy, density, region, gamma_table,
            jnp.asarray(z_matrix(cz, lanes)),
            jnp.asarray(plane_matrix(cx, cy)),
            jnp.asarray(weave_matrix(cz, lanes)),
        )

    in_specs = (P(*AXES), P(*AXES), P(*AXES), P())
    out_specs = (P(None, *AXES), P(None, *AXES))
    return jax.shard_map(
        on_device, mesh=mesh, in_specs=in_specs, out_specs=out_specs, check_vma=False
    )
```

```python
import functools
import math

import jax
import jax.numpy as jnp
import numpy as np
from jax import lax
from jax.experimental import pallas as pl
from jax.experimental.pallas import tpu as pltpu
from jax.sharding import PartitionSpec as P

MESH = pl.DeviceIdType.MESH
AXES = ("gx", "gy", "gz")
WEIGHTS = [5.0 / 18.0, 8.0 / 18.0, 5.0 / 18.0]
SUB = 8
PHASES = 3
LOW, HIGH = 2, 1
STRIDE = 4
PACKED = 128 // STRIDE


def line_tables():
    root = math.sqrt(0.15)
    spots = [0.5 - root, 0.5, 0.5 + root]
    values = [
        [2.0 * (spot - 0.5) * (spot - 1.0), -4.0 * spot * (spot - 1.0), 2.0 * spot * (spot - 0.5)]
        for spot in spots
    ]
    slopes = [[4.0 * spot - 3.0, -8.0 * spot + 4.0, 4.0 * spot - 1.0] for spot in spots]
    return np.array(values), np.array(slopes)


def line_mass():
    values, _ = line_tables()
    return values.T @ np.diag(WEIGHTS) @ values


def z_matrix(cz, lanes):
    values, slopes = line_tables()
    out = np.zeros((3 * cz, 6, lanes), np.float32)
    for k in range(3):
        for a in range(3):
            for e in range(cz):
                out[3 * e + a, k, LOW + e] = WEIGHTS[a] * values[a][k]
                out[3 * e + a, 3 + k, LOW + e] = WEIGHTS[a] * slopes[a][k]
    return out.reshape(3 * cz, 6 * lanes)


def line_matrix(count, table):
    out = np.zeros((2 * count + 1, 3 * count))
    for i in range(count):
        for a in range(3):
            for k in range(3):
                out[2 * i + k, 3 * i + a] += WEIGHTS[a] * table[a][k]
    return out


def plane_matrix(cx, cy):
    values, slopes = line_tables()
    vx, sx = line_matrix(cx, values), line_matrix(cx, slopes)
    vy, sy = line_matrix(cy, values), line_matrix(cy, slopes)
    nx, ny, points = 2 * cx + 1, 2 * cy + 1, 9 * cx * cy
    out = np.zeros((ny, nx, SUB, 2, points), np.float32)
    for c, (mx, my, part) in enumerate(((sx, vy, 0), (vx, sy, 0), (vx, vy, 1))):
        block = np.einsum("xp,yq->yxpq", mx, my).reshape(ny, nx, points)
        out[:, :, c, part] = block
        out[:, :, c + 4, part] = block
    return out.reshape(ny * nx * SUB, 2 * points)


def weave_matrix(cz, lanes):
    out = np.zeros((2, lanes, 2 * cz), np.float32)
    for e in range(cz):
        out[0, LOW + e, 2 * e] = 1.0
        out[1, LOW + e, 2 * e + 1] = 1.0
    return out.reshape(2 * lanes, 2 * cz)


def exact_dot(a, b):
    return jnp.dot(a, b, precision=lax.Precision.HIGHEST, preferred_element_type=jnp.float32)


def reduction_stages(sizes):
    return [(0, 1), (2,)]


def message_tiles(cx, cy):
    return (2 * cx + 1) * (2 * cy + 1) + -(-cx * cy // SUB)


def group_size(stage, sizes):
    return math.prod(sizes[axis] for axis in stage)


def axis_directions(index, size):
    if size == 1:
        return []
    if size == 2:
        return [(0, 0, 1 - 2 * index, None)]
    return [(0, 1, -1, index > 0), (1, 0, 1, index < size - 1)]


def pick(step, low, high):
    if isinstance(step, int):
        return low if step < 0 else high
    return jnp.where(step > 0, high, low)


def repeat(size, action):
    if size <= 8:
        for offset in range(1, size):
            action(offset)
    else:
        pl.loop(1, size)(action)


def under(conditions, action):
    conditions = [c for c in conditions if c is not None]
    if not conditions:
        action()
        return
    both = conditions[0]
    for c in conditions[1:]:
        both = jnp.logical_and(both, c)
    pl.when(both)(action)


def kernel(
    sizes, cx, cy, cz, lanes,
    energy_hbm, density_hbm, region_hbm, gamma_hbm, z_hbm, plane_hbm, weave_hbm,
    acc_out, res_out,
    energy, density, region, gamma, z_mat, plane_mat, weave_mat, load_sem,
    points, fac, fac_points, dens, part, full, rows, z_part, x_buf, y_buf, xy_buf, z_buf,
    send_sem, recv_sem, z_send, z_recv, *stage_refs,
):
    loads = [
        pltpu.make_async_copy(src, dst, load_sem.at[number])
        for number, (src, dst) in enumerate((
            (energy_hbm, energy), (density_hbm, density), (region_hbm, region), (gamma_hbm, gamma),
            (z_hbm, z_mat), (plane_hbm, plane_mat), (weave_hbm, weave_mat),
        ))
    ]
    for load in loads:
        load.start()
    nx, ny = 2 * cx + 1, 2 * cy + 1
    nodes = nx * ny
    place = [lax.axis_index(name) for name in AXES]
    stages = reduction_stages(sizes)
    centre = (2, 2, 0, None)
    dirs = [axis_directions(place[axis], sizes[axis]) for axis in range(3)]

    def target(step_x, step_y, step_z):
        return (place[0] + step_x, place[1] + step_y, place[2] + step_z)

    def partner(stage, offset):
        mine = 0
        for axis in stage:
            mine = mine * sizes[axis] + place[axis]
        other = lax.rem(mine + offset, group_size(stage, sizes))
        where = list(place)
        for axis in reversed(stage):
            where[axis] = lax.rem(other, sizes[axis])
            other = lax.div(other, sizes[axis])
        return tuple(where), mine

    for ref in (x_buf, y_buf, xy_buf, z_buf):
        ref[...] = jnp.zeros_like(ref)

    barrier = pltpu.get_barrier_semaphore()
    for stage in stages:
        size = group_size(stage, sizes)

        def greet(offset, stage=stage):
            where, _ = partner(stage, offset)
            pl.semaphore_signal(barrier, inc=1, device_id=where, device_id_type=MESH)

        repeat(size, greet)

    for load in loads[:5]:
        load.wait()
    for xp in range(3 * cx):
        points[pl.ds(xp * 3 * cy, 3 * cy), :] = energy[xp]
    gamma_elem = jnp.zeros(region.shape, jnp.float32)
    for index in range(gamma.shape[0]):
        gamma_elem = gamma_elem + jnp.where(region[...] == index, gamma[index], 0.0)
    factor = (gamma_elem - 1.0) * density[...]
    fac[...] = jnp.zeros_like(fac)
    dens[...] = jnp.zeros_like(dens)
    for i in range(cx):
        fac[pl.ds(i * cy, cy), pl.ds(LOW, cz)] = factor[i]
        dens[pl.ds(i * cy, cy), pl.ds(LOW, cz)] = density[i]
    for xp in range(3 * cx):
        for k in range(cy):
            row = fac[pl.ds((xp // 3) * cy + k, 1), :]
            fac_points[pl.ds(xp * 3 * cy + 3 * k, 3), :] = jnp.broadcast_to(row, (3, lanes))
    sums = exact_dot(points[...], z_mat[...])
    scaled = [sums[:, k * lanes : (k + 1) * lanes] * fac_points[...] for k in range(6)]
    even = jnp.concatenate(
        [scaled[0] + pltpu.roll(scaled[2], 1, 1), scaled[3] + pltpu.roll(scaled[5], 1, 1)], axis=0
    )
    odd = jnp.concatenate([scaled[1], scaled[4]], axis=0)
    loads[5].wait()
    force = exact_dot(plane_mat[...], jnp.concatenate([even, odd], axis=1))
    sub = lax.broadcasted_iota(jnp.int32, (1, SUB, lanes), 1)
    lane = lax.broadcasted_iota(jnp.int32, (1, SUB, lanes), 2)
    is_even = sub < 4
    e_part = force[:, :lanes].reshape(nodes, SUB, lanes)
    o_part = force[:, lanes:].reshape(nodes, SUB, lanes)
    part[0] = jnp.where(is_even, e_part, o_part).reshape(ny, nx, SUB, lanes)

    top = LOW + cz
    used = jnp.logical_and(
        lax.rem(sub, 4) < 3, lane < jnp.where(is_even, top + HIGH + 1, top + HIGH)
    )
    wall_low = jnp.logical_and(place[2] == 0, jnp.logical_and(is_even, lane == LOW))
    wall_high = jnp.logical_and(
        place[2] == sizes[2] - 1, jnp.logical_and(is_even, lane == top)
    )
    keep = jnp.where(
        jnp.logical_and(used, jnp.logical_not(jnp.logical_or(wall_low, wall_high))), 1.0, 0.0
    )
    owned = jnp.where(jnp.logical_and(lane >= LOW, lane < top), 1.0, 0.0)

    flat_lane = lax.broadcasted_iota(jnp.int32, (SUB, lanes), 1)
    density_tiles = -(-cx * cy // SUB)

    def tile_of(number):
        if number < nodes:
            return part[0, number // nx, number % nx]
        return dens[pl.ds((number - nodes) * SUB, SUB), :]

    spans = ((LOW, top, HIGH + 1), (top - LOW, 0, LOW + 1))

    def pack_z():
        for side, (first, _, width) in enumerate(spans):
            for group in range(-(-(nodes + density_tiles) // PACKED)):
                tile = jnp.zeros((SUB, lanes), jnp.float32)
                for number in range(group * PACKED, min((group + 1) * PACKED, nodes + density_tiles)):
                    at = STRIDE * (number % PACKED)
                    moved = pltpu.roll(tile_of(number), (at - first) % lanes, 1)
                    hot = jnp.logical_and(flat_lane >= at, flat_lane < at + width)
                    tile = tile + jnp.where(hot, moved, 0.0)
                z_part[side, group] = tile

    def copy_z(side_z, arriving):
        sz, tz, dz, _ = side_z
        own, src = z_buf.at[sz], z_part.at[pick(dz, 0, 1)]
        return pltpu.make_async_remote_copy(
            src_ref=src, dst_ref=own if arriving else z_buf.at[tz],
            send_sem=z_send.at[sz], recv_sem=z_recv.at[sz if arriving else tz],
            device_id=target(0, 0, dz), device_id_type=MESH,
        )

    def exchange_z():
        pack_z()
        for side_z in dirs[2]:
            under([side_z[3]], lambda side_z=side_z: copy_z(side_z, False).start())
        for side_z in dirs[2]:
            under([side_z[3]], lambda side_z=side_z: copy_z(side_z, True).wait_recv())
        arrived = []
        for side_z in dirs[2]:
            sz, _, dz, _ = side_z
            arrived.append((sz, pick(dz, 0, top), pick(dz, LOW + 1, HIGH + 1)))
        for number in range(nodes + density_tiles):
            group, at = divmod(number, PACKED)
            tile = tile_of(number)
            for sz, first, width in arrived:
                shift = first - STRIDE * at
                shift = shift % lanes if isinstance(shift, int) else lax.rem(shift + lanes, lanes)
                moved = pltpu.roll(z_buf[sz, group], shift, 1)
                hot = jnp.logical_and(flat_lane >= first, flat_lane < first + width)
                tile = tile + jnp.where(hot, moved, 0.0)
            if number < nodes:
                part[0, number // nx, number % nx] = tile
            else:
                dens[pl.ds((number - nodes) * SUB, SUB), :] = tile

    def copies(phase, side_x, side_y):
        (sx, tx, dx, _), (sy, ty, dy, _) = side_x, side_y
        here, there = [phase * 9 + a * 3 + b for a, b in ((sx, sy), (tx, ty))]
        xf, yf = pick(dx, 0, nx - 1), pick(dy, 0, ny - 1)
        if sy == 2:
            src = part.at[phase, :, xf]
            dst, own = x_buf.at[phase, tx], x_buf.at[phase, sx]
        elif sx == 2:
            src = part.at[phase, yf]
            dst, own = y_buf.at[phase, ty], y_buf.at[phase, sy]
        else:
            src = part.at[phase, yf, xf]
            dst, own = xy_buf.at[phase, tx, ty], xy_buf.at[phase, sx, sy]

        def make(dst_ref, slot):
            return pltpu.make_async_remote_copy(
                src_ref=src, dst_ref=dst_ref, send_sem=send_sem.at[here], recv_sem=recv_sem.at[slot],
                device_id=target(dx, dy, 0), device_id_type=MESH,
            )

        return lambda: make(dst, there), lambda: make(own, here)

    def facing(axis, step):
        chosen = []
        for direction in dirs[axis]:
            slot, at, own_step, there = direction
            if step is None:
                chosen.append(direction)
            elif isinstance(own_step, int):
                if own_step == step:
                    chosen.append(direction)
            else:
                chosen.append((slot, at, step, own_step == step))
        return chosen + [centre]

    def each(phase, step, action):
        if phase + 1 < PHASES:
            step = None
        groups = {}
        for side_x in facing(0, step):
            for side_y in facing(1, step):
                if side_x[0] == 2 and side_y[0] == 2:
                    continue
                conditions = (side_x[3], side_y[3])
                key = tuple(None if c is None else d[0] for c, d in zip(conditions, (side_x, side_y)))
                groups.setdefault(key, (conditions, []))[1].append((side_x, side_y))
        for conditions, members in groups.values():

            def run(members=members):
                for member in members:
                    action(copies(phase, *member))

            under(conditions, run)

    def start(phase):
        each(phase, 1, lambda pair: pair[0]().start())

    def finish(phase):
        each(phase, -1, lambda pair: pair[1]().wait_recv())
        full[phase] = part[phase] * keep.reshape(1, 1, SUB, lanes)
        for sx, _, dx, _ in dirs[0]:
            xf = pick(dx, 0, nx - 1)
            full[phase, :, xf] = full[phase, :, xf] + x_buf[phase, sx] * keep
        for sy, _, dy, _ in dirs[1]:
            yf = pick(dy, 0, ny - 1)
            full[phase, yf] = full[phase, yf] + y_buf[phase, sy] * keep
            for sx, _, dx, _ in dirs[0]:
                xf = pick(dx, 0, nx - 1)
                full[phase, yf, xf] = full[phase, yf, xf] + xy_buf[phase, sx, sy] * keep[0]
        for axis, last in ((0, nx - 1), (1, ny - 1)):
            for at, here in ((0, place[axis] == 0), (last, place[axis] == sizes[axis] - 1)):

                @pl.when(here)
                def _(axis=axis, at=at):
                    if axis == 0:
                        full[phase, :, at] = jnp.zeros((ny, SUB, lanes), jnp.float32)
                    else:
                        full[phase, at] = jnp.zeros((nx, SUB, lanes), jnp.float32)

    mass = [[float(v) for v in line] for line in line_mass()]

    def combine(weights, parts):
        return weights[0] * parts[0] + weights[1] * parts[1] + weights[2] * parts[2]

    on_even, on_odd, on_next = [
        jnp.where(is_even, mass[0][k], mass[1][k]).astype(jnp.float32) for k in range(3)
    ]
    even_only = jnp.where(is_even, 1.0, 0.0)

    def apply_mass(source, phase):
        lines = [full[source, y] for y in range(ny)]
        along_y = jnp.concatenate(
            [combine(mass[l], lines[2 * k : 2 * k + 3])[None] for k in range(cy) for l in range(3)],
            axis=0,
        )
        at_x = [along_y[:, x] for x in range(nx)]
        blocks = []
        for i in range(cx):
            tiles = [
                jnp.broadcast_to(dens[pl.ds(i * cy + k, 1), :], (SUB, lanes))[None]
                for k in range(cy)
                for _ in range(3)
            ]
            rho = jnp.concatenate(tiles, axis=0)
            rho_next = rho * even_only
            for j in range(3):
                t = combine(mass[j], at_x[2 * i : 2 * i + 3])
                other = pltpu.roll(t, 4, 1)
                evens, odds = jnp.where(is_even, t, other), jnp.where(is_even, other, t)
                following = pltpu.roll(evens, lanes - 1, 2)
                own = on_even * evens + on_odd * odds + on_next * following
                far = combine(mass[2], (evens, odds, following))
                blocks.append(rho * own + pltpu.roll(rho_next * far, 1, 2))
        for x in range(nx):
            i, odd_x = divmod(x, 2)
            if odd_x:
                column = blocks[3 * i + 1]
            elif x == 0:
                column = blocks[0]
            elif x == nx - 1:
                column = blocks[3 * i - 1]
            else:
                column = blocks[3 * i] + blocks[3 * i - 1]
            for y in range(ny):
                k, odd_y = divmod(y, 2)
                if odd_y:
                    value = column[3 * k + 1]
                elif y == 0:
                    value = column[0]
                elif y == ny - 1:
                    value = column[3 * k - 1]
                else:
                    value = column[3 * k] + column[3 * k - 1]
                part[phase, y, x] = value

    def woven(phase):
        rows[...] = full[phase].reshape(nodes * SUB, lanes)
        halves = []
        for first in (0, 4):
            halves.append(jnp.concatenate(
                [
                    rows[pl.ds(x * SUB + first + c, 2 * cy, stride=nx * SUB), :]
                    for c in range(3)
                    for x in range(2 * cx)
                ],
                axis=0,
            ))
        return exact_dot(jnp.concatenate(halves, axis=1), weave_mat[...])

    if sum(group_size(stage, sizes) - 1 for stage in stages):
        pl.semaphore_wait(barrier, sum(group_size(stage, sizes) - 1 for stage in stages))
    exchange_z()
    start(0)
    finish(0)
    apply_mass(0, 1)
    start(1)
    finish(1)
    apply_mass(1, 2)
    start(2)

    force_own = full[0, : ny - 1, : nx - 1].reshape(4 * cx * cy, SUB, lanes) * owned
    image_own = full[1, : ny - 1, : nx - 1].reshape(4 * cx * cy, SUB, lanes) * owned
    products = [
        jnp.sum(force_own * force_own, axis=0),
        jnp.sum(force_own * image_own, axis=0),
        jnp.sum(image_own * image_own, axis=0),
        jnp.sum((full[1] * part[2]).reshape(nodes, SUB, lanes) * owned, axis=0),
    ]
    flat_sub = lax.broadcasted_iota(jnp.int32, (SUB, 128), 0)
    message = jnp.zeros((SUB, 128), jnp.float32)
    for k, product in enumerate(products):
        hot = flat_lane == 4 * lax.rem(flat_sub, 4) + k
        message = message + jnp.where(hot, jnp.sum(product, axis=1, keepdims=True), 0.0)
    total = jnp.sum(message, axis=0, keepdims=True)

    loads[6].wait()
    for number, stage in enumerate(stages):
        slots, stage_send, stage_recv = stage_refs[3 * number : 3 * number + 3]
        size = group_size(stage, sizes)
        if size > 1:
            _, mine = partner(stage, 0)
            slots[mine] = total

            def copy_to(offset, stage=stage, slots=slots, sems=(stage_send, stage_recv)):
                where, at = partner(stage, offset)
                pltpu.make_async_remote_copy(
                    src_ref=slots.at[at], dst_ref=slots.at[at], send_sem=sems[0], recv_sem=sems[1],
                    device_id=where, device_id_type=MESH,
                ).start()

            repeat(size, copy_to)
        if number == 0:
            woven_force, woven_image = woven(0), woven(1)
        elif number == 1:
            finish(2)
            woven_second = woven(2)
        if size > 1:
            where, _ = partner(stage, 1)
            others = slots.at[pl.ds(0, size - 1)]
            wait = pltpu.make_async_remote_copy(
                src_ref=others, dst_ref=others, send_sem=stage_send, recv_sem=stage_recv,
                device_id=where, device_id_type=MESH,
            )
            wait.wait_recv()
            wait.wait_send()
            total = jnp.sum(slots[...], axis=0)

    row_lane = lax.broadcasted_iota(jnp.int32, (1, 128), 1)
    live = jnp.logical_and(lax.rem(row_lane, 4) == 0, row_lane < 12)
    ff, fi, ii, si = [
        jnp.where(live, total if k == 0 else pltpu.roll(total, 128 - k, 1), 1.0) for k in range(4)
    ]
    alpha = ff / fi
    next_norm = alpha * alpha * ii - ff
    ratio = next_norm / ff
    curvature = fi - 2.0 * alpha * ii + alpha * alpha * si - ratio * next_norm / alpha
    second = next_norm / curvature
    outer = alpha + second * (1.0 + ratio)
    inner = alpha * second
    per = 2 * cx * 2 * cy
    for c in range(3):
        hot = row_lane == 4 * c
        a = jnp.sum(jnp.where(hot, outer, 0.0), axis=1, keepdims=True)
        b = jnp.sum(jnp.where(hot, inner, 0.0), axis=1, keepdims=True)
        here = slice(c * per, (c + 1) * per)
        f, q, s = woven_force[here], woven_image[here], woven_second[here]
        acc_out[c] = (a * f - b * q).reshape(2 * cx, 2 * cy, 2 * cz)
        res_out[c] = (f - a * q + b * s).reshape(2 * cx, 2 * cy, 2 * cz)

    for side_z in dirs[2]:
        under([side_z[3]], lambda side_z=side_z: copy_z(side_z, False).wait_send())
    for phase in range(PHASES):
        each(phase, 1, lambda pair: pair[0]().wait_send())


def solution(mesh):
    sizes = tuple(mesh.shape[name] for name in AXES)

    def on_device(energy, density, region, gamma_table):
        cx, cy, cz = density.shape
        lanes = -(-(cz + LOW + HIGH + 1) // 128) * 128
        nx, ny = 2 * cx + 1, 2 * cy + 1
        out = jax.ShapeDtypeStruct((3, 2 * cx, 2 * cy, 2 * cz), jnp.float32)
        vmem = pl.BlockSpec(memory_space=pltpu.VMEM)
        hbm = pl.BlockSpec(memory_space=pltpu.HBM)
        tables = [z_matrix(cz, lanes), plane_matrix(cx, cy), weave_matrix(cz, lanes)]
        groups = -(-message_tiles(cx, cy) // PACKED)
        tile = (SUB, lanes)
        scratch = [
            pltpu.VMEM(energy.shape, jnp.float32),
            pltpu.VMEM(density.shape, jnp.float32),
            pltpu.VMEM(region.shape, jnp.int32),
            pltpu.SMEM(gamma_table.shape, jnp.float32),
            *[pltpu.VMEM(table.shape, jnp.float32) for table in tables],
            pltpu.SemaphoreType.DMA((7,)),
            pltpu.VMEM((9 * cx * cy, 3 * cz), jnp.float32),
            pltpu.VMEM((cx * cy, lanes), jnp.float32),
            pltpu.VMEM((9 * cx * cy, lanes), jnp.float32),
            pltpu.VMEM((-(-cx * cy // SUB) * SUB, lanes), jnp.float32),
            pltpu.VMEM((PHASES, ny, nx) + tile, jnp.float32),
            pltpu.VMEM((PHASES, ny, nx) + tile, jnp.float32),
            pltpu.VMEM((ny * nx * SUB, lanes), jnp.float32),
            pltpu.VMEM((2, groups) + tile, jnp.float32),
            pltpu.VMEM((PHASES, 2, ny) + tile, jnp.float32),
            pltpu.VMEM((PHASES, 2, nx) + tile, jnp.float32),
            pltpu.VMEM((PHASES, 2, 2) + tile, jnp.float32),
            pltpu.VMEM((2, groups) + tile, jnp.float32),
            pltpu.SemaphoreType.DMA((PHASES * 9,)),
            pltpu.SemaphoreType.DMA((PHASES * 9,)),
            pltpu.SemaphoreType.DMA((2,)),
            pltpu.SemaphoreType.DMA((2,)),
        ]
        for stage in reduction_stages(sizes):
            scratch += [
                pltpu.VMEM((group_size(stage, sizes), 1, 128), jnp.float32),
                pltpu.SemaphoreType.DMA,
                pltpu.SemaphoreType.DMA,
            ]
        return pl.pallas_call(
            functools.partial(kernel, sizes, cx, cy, cz, lanes),
            out_shape=(out, out),
            in_specs=[hbm] * 7,
            out_specs=(vmem, vmem),
            scratch_shapes=scratch,
            compiler_params=pltpu.CompilerParams(
                collective_id=0, has_side_effects=True, vmem_limit_bytes=60 * 1024 * 1024
            ),
        )(
            energy, density, region, gamma_table, *[jnp.asarray(table) for table in tables],
        )

    in_specs = (P(*AXES), P(*AXES), P(*AXES), P())
    out_specs = (P(None, *AXES), P(None, *AXES))
    return jax.shard_map(
        on_device, mesh=mesh, in_specs=in_specs, out_specs=out_specs, check_vma=False
    )
```

```python
import functools
import math

import jax
import jax.numpy as jnp
import numpy as np
from jax import lax
from jax.experimental import pallas as pl
from jax.experimental.pallas import tpu as pltpu
from jax.sharding import PartitionSpec as P

MESH = pl.DeviceIdType.MESH
AXES = ("gx", "gy", "gz")
WEIGHTS = [5.0 / 18.0, 8.0 / 18.0, 5.0 / 18.0]
SUB = 8
PHASES = 3
LOW, HIGH = 2, 1
STRIDE = 4
PACKED = 128 // STRIDE


def line_tables():
    root = math.sqrt(0.15)
    spots = [0.5 - root, 0.5, 0.5 + root]
    values = [
        [2.0 * (spot - 0.5) * (spot - 1.0), -4.0 * spot * (spot - 1.0), 2.0 * spot * (spot - 0.5)]
        for spot in spots
    ]
    slopes = [[4.0 * spot - 3.0, -8.0 * spot + 4.0, 4.0 * spot - 1.0] for spot in spots]
    return np.array(values), np.array(slopes)


def line_mass():
    values, _ = line_tables()
    return values.T @ np.diag(WEIGHTS) @ values


def z_matrix(cz, lanes):
    values, slopes = line_tables()
    out = np.zeros((3 * cz, 6, lanes), np.float32)
    for k in range(3):
        for a in range(3):
            for e in range(cz):
                out[3 * e + a, k, LOW + e] = WEIGHTS[a] * values[a][k]
                out[3 * e + a, 3 + k, LOW + e] = WEIGHTS[a] * slopes[a][k]
    return out.reshape(3 * cz, 6 * lanes)


def line_matrix(count, table):
    out = np.zeros((2 * count + 1, 3 * count))
    for i in range(count):
        for a in range(3):
            for k in range(3):
                out[2 * i + k, 3 * i + a] += WEIGHTS[a] * table[a][k]
    return out


def plane_matrix(cx, cy):
    values, slopes = line_tables()
    vx, sx = line_matrix(cx, values), line_matrix(cx, slopes)
    vy, sy = line_matrix(cy, values), line_matrix(cy, slopes)
    nx, ny, points = 2 * cx + 1, 2 * cy + 1, 9 * cx * cy
    out = np.zeros((ny, nx, SUB, 2, -(-points // 16) * 16), np.float32)
    for c, (mx, my, part) in enumerate(((sx, vy, 0), (vx, sy, 0), (vx, vy, 1))):
        block = np.einsum("xp,yq->yxpq", mx, my).reshape(ny, nx, points)
        out[:, :, c, part, :points] = block
        out[:, :, c + 4, part, :points] = block
    return out.reshape(ny * nx * SUB, -1)


def weave_matrix(cz, lanes):
    out = np.zeros((2, lanes, 2 * cz), np.float32)
    for e in range(cz):
        out[0, LOW + e, 2 * e] = 1.0
        out[1, LOW + e, 2 * e + 1] = 1.0
    return out.reshape(2 * lanes, 2 * cz)


def halves(array):
    parts = []
    rest = array
    for _ in range(3):
        piece = rest.astype(jnp.bfloat16)
        parts.append(piece)
        rest = rest - piece.astype(jnp.float32)
    return parts


def padded_rows(table):
    rows = -(-table.shape[0] // 16) * 16
    return np.pad(table, ((0, rows - table.shape[0]), (0, 0)))


def dot(a, b):
    return jnp.dot(a, b, preferred_element_type=jnp.float32)


def by_parts(left, right, count):
    first = dot(jnp.concatenate(left, axis=0), right[0])
    second = dot(jnp.concatenate(left[:2], axis=0), right[1])
    third = dot(left[0], right[2])
    small = first[2 * count :] + second[count:] + third
    return first[:count] + (first[count : 2 * count] + second[:count] + small)


def reduction_stages(sizes):
    return [(0, 1, 2)] if math.prod(sizes) <= 64 else [(0, 1), (2,)]


def message_tiles(cx, cy):
    return (2 * cx + 1) * (2 * cy + 1) + -(-cx * cy // SUB)


def group_size(stage, sizes):
    return math.prod(sizes[axis] for axis in stage)


def axis_directions(index, size):
    if size == 1:
        return []
    if size == 2:
        return [(0, 0, 1 - 2 * index, None)]
    return [(0, 1, -1, index > 0), (1, 0, 1, index < size - 1)]


def pick(step, low, high):
    if isinstance(step, int):
        return low if step < 0 else high
    return jnp.where(step > 0, high, low)


def repeat(size, action):
    if size <= 64:
        for offset in range(1, size):
            action(offset)
    else:
        pl.loop(1, size)(action)


def under(conditions, action):
    conditions = [c for c in conditions if c is not None]
    if not conditions:
        action()
        return
    both = conditions[0]
    for c in conditions[1:]:
        both = jnp.logical_and(both, c)
    pl.when(both)(action)


def kernel(
    sizes, cx, cy, cz, lanes,
    energy_hbm, density_hbm, region_hbm, gamma_hbm, z_hbm, plane_hbm, weave_hbm,
    acc_out, res_out,
    energy, density, region, gamma, z_mat, plane_mat, weave_mat, load_sem,
    points, fac, fac_points, dens, part, full, rows, z_part, x_buf, y_buf, xy_buf, z_buf,
    send_sem, recv_sem, z_send, z_recv, *stage_refs,
):
    loads = [
        pltpu.make_async_copy(src, dst, load_sem.at[number])
        for number, (src, dst) in enumerate((
            (energy_hbm, energy), (density_hbm, density), (region_hbm, region), (gamma_hbm, gamma),
            (z_hbm, z_mat), (plane_hbm, plane_mat), (weave_hbm, weave_mat),
        ))
    ]
    for load in loads:
        load.start()
    nx, ny = 2 * cx + 1, 2 * cy + 1
    nodes = nx * ny
    place = [lax.axis_index(name) for name in AXES]
    stages = reduction_stages(sizes)
    centre = (2, 2, 0, None)
    dirs = [axis_directions(place[axis], sizes[axis]) for axis in range(3)]

    def target(step_x, step_y, step_z):
        return (place[0] + step_x, place[1] + step_y, place[2] + step_z)

    def partner(stage, offset):
        mine = 0
        where = list(place)
        for axis in stage:
            mine = mine * sizes[axis] + place[axis]
        for axis in reversed(stage):
            if isinstance(offset, int):
                offset, step = divmod(offset, sizes[axis])
            else:
                offset, step = lax.div(offset, sizes[axis]), lax.rem(offset, sizes[axis])
            at = place[axis] + step
            where[axis] = jnp.where(at >= sizes[axis], at - sizes[axis], at)
        return tuple(where), mine

    for ref in (x_buf, y_buf, xy_buf, z_buf):
        ref[...] = jnp.zeros_like(ref)

    barrier = pltpu.get_barrier_semaphore()
    for stage in stages:
        size = group_size(stage, sizes)

        def greet(offset, stage=stage):
            where, _ = partner(stage, offset)
            pl.semaphore_signal(barrier, inc=1, device_id=where, device_id_type=MESH)

        repeat(size, greet)

    for load in loads[:5]:
        load.wait()
    used_points = 9 * cx * cy
    if points.shape[0] > used_points:
        spare = points.shape[0] - used_points
        points[pl.ds(used_points, spare), :] = jnp.zeros((spare, 3 * cz), jnp.float32)
        fac_points[pl.ds(used_points, spare), :] = jnp.zeros((spare, lanes), jnp.float32)
    for xp in range(3 * cx):
        points[pl.ds(xp * 3 * cy, 3 * cy), :] = energy[xp]
    gamma_elem = jnp.zeros(region.shape, jnp.float32)
    for index in range(gamma.shape[0]):
        gamma_elem = gamma_elem + jnp.where(region[...] == index, gamma[index], 0.0)
    factor = (gamma_elem - 1.0) * density[...]
    fac[...] = jnp.zeros_like(fac)
    dens[...] = jnp.zeros_like(dens)
    for i in range(cx):
        fac[pl.ds(i * cy, cy), pl.ds(LOW, cz)] = factor[i]
        dens[pl.ds(i * cy, cy), pl.ds(LOW, cz)] = density[i]
    for xp in range(3 * cx):
        for k in range(cy):
            row = fac[pl.ds((xp // 3) * cy + k, 1), :]
            fac_points[pl.ds(xp * 3 * cy + 3 * k, 3), :] = jnp.broadcast_to(row, (3, lanes))
    point_rows = points.shape[0]
    sums = by_parts(halves(points[...]), halves(z_mat[...]), point_rows)
    scaled = [sums[:, k * lanes : (k + 1) * lanes] * fac_points[...] for k in range(6)]
    even = jnp.concatenate(
        [scaled[0] + pltpu.roll(scaled[2], 1, 1), scaled[3] + pltpu.roll(scaled[5], 1, 1)], axis=0
    )
    odd = jnp.concatenate([scaled[1], scaled[4]], axis=0)
    loads[5].wait()
    force = by_parts(
        halves(plane_mat[...]),
        halves(jnp.concatenate([even, odd], axis=1)),
        plane_mat.shape[0],
    )[: nodes * SUB]
    sub = lax.broadcasted_iota(jnp.int32, (1, SUB, lanes), 1)
    lane = lax.broadcasted_iota(jnp.int32, (1, SUB, lanes), 2)
    is_even = sub < 4
    e_part = force[:, :lanes].reshape(nodes, SUB, lanes)
    o_part = force[:, lanes:].reshape(nodes, SUB, lanes)
    part[0] = jnp.where(is_even, e_part, o_part).reshape(ny, nx, SUB, lanes)

    top = LOW + cz
    used = jnp.logical_and(
        lax.rem(sub, 4) < 3, lane < jnp.where(is_even, top + HIGH + 1, top + HIGH)
    )
    wall_low = jnp.logical_and(place[2] == 0, jnp.logical_and(is_even, lane == LOW))
    wall_high = jnp.logical_and(
        place[2] == sizes[2] - 1, jnp.logical_and(is_even, lane == top)
    )
    keep = jnp.where(
        jnp.logical_and(used, jnp.logical_not(jnp.logical_or(wall_low, wall_high))), 1.0, 0.0
    )
    owned = jnp.where(jnp.logical_and(lane >= LOW, lane < top), 1.0, 0.0)

    flat_lane = lax.broadcasted_iota(jnp.int32, (SUB, lanes), 1)
    density_tiles = -(-cx * cy // SUB)

    def tile_of(number):
        if number < nodes:
            return part[0, number // nx, number % nx]
        return dens[pl.ds((number - nodes) * SUB, SUB), :]

    spans = ((LOW, top, HIGH + 1), (top - LOW, 0, LOW + 1))

    def pack_z():
        for side, (first, _, width) in enumerate(spans):
            for group in range(-(-(nodes + density_tiles) // PACKED)):
                tile = jnp.zeros((SUB, lanes), jnp.float32)
                for number in range(group * PACKED, min((group + 1) * PACKED, nodes + density_tiles)):
                    at = STRIDE * (number % PACKED)
                    moved = pltpu.roll(tile_of(number), (at - first) % lanes, 1)
                    hot = jnp.logical_and(flat_lane >= at, flat_lane < at + width)
                    tile = tile + jnp.where(hot, moved, 0.0)
                z_part[side, group] = tile

    def copy_z(side_z, side_x, side_y, arriving):
        (sx, tx, dx, _), (sy, ty, dy, _), (sz, tz, dz, _) = side_x, side_y, side_z
        here, there = [(c * 3 + a) * 3 + b for a, b, c in ((sx, sy, sz), (tx, ty, tz))]
        return pltpu.make_async_remote_copy(
            src_ref=z_part.at[pick(dz, 0, 1)],
            dst_ref=z_buf.at[sz, sx, sy] if arriving else z_buf.at[tz, tx, ty],
            send_sem=z_send.at[here], recv_sem=z_recv.at[here if arriving else there],
            device_id=target(dx, dy, dz), device_id_type=MESH,
        )

    def each_z(action):
        for side_z in dirs[2]:
            for side_x in dirs[0] + [centre]:
                ys = dirs[1] + [centre]
                free = [side_y for side_y in ys if side_y[3] is None]

                def run(side_z=side_z, side_x=side_x, free=free):
                    for side_y in free:
                        action(side_z, side_x, side_y)

                under([side_z[3], side_x[3]], run)
                for side_y in ys:
                    if side_y[3] is not None:
                        under(
                            [side_z[3], side_x[3], side_y[3]],
                            lambda a=side_z, b=side_x, c=side_y: action(a, b, c),
                        )

    def piece_z(side_z, sx, sy, number):
        sz, _, dz, _ = side_z
        first, width = pick(dz, 0, top), pick(dz, LOW + 1, HIGH + 1)
        if isinstance(number, int):
            group, at = divmod(number, PACKED)
        else:
            group, at = lax.div(number, PACKED), lax.rem(number, PACKED)
        shift = first - STRIDE * at
        shift = shift % lanes if isinstance(shift, int) else lax.rem(shift + lanes, lanes)
        moved = pltpu.roll(z_buf[sz, sx, sy, group], shift, 1)
        return jnp.where(jnp.logical_and(flat_lane >= first, flat_lane < first + width), moved, 0.0)

    def add_z():
        each_z(lambda a, b, c: copy_z(a, b, c, True).wait_recv())
        for number in range(nodes + density_tiles):
            if number < nodes:
                tile = full[0, number // nx, number % nx]
            else:
                tile = dens[pl.ds((number - nodes) * SUB, SUB), :]
            for side_z in dirs[2]:
                tile = tile + piece_z(side_z, 2, 2, number)
            if number < nodes:
                full[0, number // nx, number % nx] = tile
            else:
                dens[pl.ds((number - nodes) * SUB, SUB), :] = tile
        for side_x in dirs[0]:
            xf, from_x = pick(side_x[2], 0, nx - 1), pick(side_x[2], nx - 1, 0)
            for y in range(ny):
                full[0, y, xf] = full[0, y, xf] + sum(
                    piece_z(side_z, side_x[0], 2, y * nx + from_x) for side_z in dirs[2]
                )
        for side_y in dirs[1]:
            yf, from_y = pick(side_y[2], 0, ny - 1), pick(side_y[2], ny - 1, 0)
            for x in range(nx):
                full[0, yf, x] = full[0, yf, x] + sum(
                    piece_z(side_z, 2, side_y[0], from_y * nx + x) for side_z in dirs[2]
                )
            for side_x in dirs[0]:
                xf, from_x = pick(side_x[2], 0, nx - 1), pick(side_x[2], nx - 1, 0)
                full[0, yf, xf] = full[0, yf, xf] + sum(
                    piece_z(side_z, side_x[0], side_y[0], from_y * nx + from_x)
                    for side_z in dirs[2]
                )

    def copies(phase, side_x, side_y):
        (sx, tx, dx, _), (sy, ty, dy, _) = side_x, side_y
        here, there = [phase * 9 + a * 3 + b for a, b in ((sx, sy), (tx, ty))]
        xf, yf = pick(dx, 0, nx - 1), pick(dy, 0, ny - 1)
        if sy == 2:
            src = part.at[phase, :, xf]
            dst, own = x_buf.at[phase, tx], x_buf.at[phase, sx]
        elif sx == 2:
            src = part.at[phase, yf]
            dst, own = y_buf.at[phase, ty], y_buf.at[phase, sy]
        else:
            src = part.at[phase, yf, xf]
            dst, own = xy_buf.at[phase, tx, ty], xy_buf.at[phase, sx, sy]

        def make(dst_ref, slot):
            return pltpu.make_async_remote_copy(
                src_ref=src, dst_ref=dst_ref, send_sem=send_sem.at[here], recv_sem=recv_sem.at[slot],
                device_id=target(dx, dy, 0), device_id_type=MESH,
            )

        return lambda: make(dst, there), lambda: make(own, here)

    def facing(axis, step):
        chosen = []
        for direction in dirs[axis]:
            slot, at, own_step, there = direction
            if step is None:
                chosen.append(direction)
            elif isinstance(own_step, int):
                if own_step == step:
                    chosen.append(direction)
            else:
                chosen.append((slot, at, step, own_step == step))
        return chosen + [centre]

    def each(phase, step, action):
        if phase + 1 < PHASES:
            step = None
        groups = {}
        for side_x in facing(0, step):
            for side_y in facing(1, step):
                if side_x[0] == 2 and side_y[0] == 2:
                    continue
                conditions = (side_x[3], side_y[3])
                key = tuple(None if c is None else d[0] for c, d in zip(conditions, (side_x, side_y)))
                groups.setdefault(key, (conditions, []))[1].append((side_x, side_y))
        for conditions, members in groups.values():

            def run(members=members):
                for member in members:
                    action(copies(phase, *member))

            under(conditions, run)

    def start(phase):
        each(phase, 1, lambda pair: pair[0]().start())

    def finish(phase):
        each(phase, -1, lambda pair: pair[1]().wait_recv())
        full[phase] = part[phase]
        for sx, _, dx, _ in dirs[0]:
            xf = pick(dx, 0, nx - 1)
            full[phase, :, xf] = full[phase, :, xf] + x_buf[phase, sx]
        for sy, _, dy, _ in dirs[1]:
            yf = pick(dy, 0, ny - 1)
            full[phase, yf] = full[phase, yf] + y_buf[phase, sy]
            for sx, _, dx, _ in dirs[0]:
                xf = pick(dx, 0, nx - 1)
                full[phase, yf, xf] = full[phase, yf, xf] + xy_buf[phase, sx, sy]
        if phase == 0 and dirs[2]:
            add_z()
        full[phase] = full[phase] * keep.reshape(1, 1, SUB, lanes)
        for axis, last in ((0, nx - 1), (1, ny - 1)):
            for at, here in ((0, place[axis] == 0), (last, place[axis] == sizes[axis] - 1)):

                @pl.when(here)
                def _(axis=axis, at=at):
                    if axis == 0:
                        full[phase, :, at] = jnp.zeros((ny, SUB, lanes), jnp.float32)
                    else:
                        full[phase, at] = jnp.zeros((nx, SUB, lanes), jnp.float32)

    mass = [[float(v) for v in line] for line in line_mass()]

    def combine(weights, parts):
        return weights[0] * parts[0] + weights[1] * parts[1] + weights[2] * parts[2]

    on_even, on_odd, on_next = [
        jnp.where(is_even, mass[0][k], mass[1][k]).astype(jnp.float32) for k in range(3)
    ]
    even_only = jnp.where(is_even, 1.0, 0.0)

    def apply_mass(source, phase):
        lines = [full[source, y] for y in range(ny)]
        along_y = jnp.concatenate(
            [combine(mass[l], lines[2 * k : 2 * k + 3])[None] for k in range(cy) for l in range(3)],
            axis=0,
        )
        at_x = [along_y[:, x] for x in range(nx)]
        blocks = []
        for i in range(cx):
            tiles = [
                jnp.broadcast_to(dens[pl.ds(i * cy + k, 1), :], (SUB, lanes))[None]
                for k in range(cy)
                for _ in range(3)
            ]
            rho = jnp.concatenate(tiles, axis=0)
            rho_next = rho * even_only
            for j in range(3):
                t = combine(mass[j], at_x[2 * i : 2 * i + 3])
                other = pltpu.roll(t, 4, 1)
                evens, odds = jnp.where(is_even, t, other), jnp.where(is_even, other, t)
                following = pltpu.roll(evens, lanes - 1, 2)
                own = on_even * evens + on_odd * odds + on_next * following
                far = combine(mass[2], (evens, odds, following))
                blocks.append(rho * own + pltpu.roll(rho_next * far, 1, 2))
        for x in range(nx):
            i, odd_x = divmod(x, 2)
            if odd_x:
                column = blocks[3 * i + 1]
            elif x == 0:
                column = blocks[0]
            elif x == nx - 1:
                column = blocks[3 * i - 1]
            else:
                column = blocks[3 * i] + blocks[3 * i - 1]
            for y in range(ny):
                k, odd_y = divmod(y, 2)
                if odd_y:
                    value = column[3 * k + 1]
                elif y == 0:
                    value = column[0]
                elif y == ny - 1:
                    value = column[3 * k - 1]
                else:
                    value = column[3 * k] + column[3 * k - 1]
                part[phase, y, x] = value

    def woven(phase):
        rows[...] = full[phase].reshape(nodes * SUB, lanes)
        sides = []
        for first in (0, 4):
            sides.append(jnp.concatenate(
                [
                    rows[pl.ds(x * SUB + first + c, 2 * cy, stride=nx * SUB), :]
                    for c in range(3)
                    for x in range(2 * cx)
                ],
                axis=0,
            ))
        wide = jnp.concatenate(sides, axis=1)
        count = wide.shape[0]
        out = dot(jnp.concatenate(halves(wide), axis=0), weave_mat[...].astype(jnp.bfloat16))
        return out[:count] + (out[count : 2 * count] + out[2 * count :])

    if sum(group_size(stage, sizes) - 1 for stage in stages):
        pl.semaphore_wait(barrier, sum(group_size(stage, sizes) - 1 for stage in stages))
    start(0)
    if dirs[2]:
        pack_z()
        each_z(lambda a, b, c: copy_z(a, b, c, False).start())
    finish(0)

    @pl.loop(0, PHASES - 1)
    def _(number):
        apply_mass(number, number + 1)

        @pl.when(number == 0)
        def _():
            start(1)
            finish(1)

    start(2)

    force_own = full[0, : ny - 1, : nx - 1].reshape(4 * cx * cy, SUB, lanes) * owned
    image_own = full[1, : ny - 1, : nx - 1].reshape(4 * cx * cy, SUB, lanes) * owned
    products = [
        jnp.sum(force_own * force_own, axis=0),
        jnp.sum(force_own * image_own, axis=0),
        jnp.sum(image_own * image_own, axis=0),
        jnp.sum((full[1] * part[2]).reshape(nodes, SUB, lanes) * owned, axis=0),
    ]
    flat_sub = lax.broadcasted_iota(jnp.int32, (SUB, 128), 0)
    message = jnp.zeros((SUB, 128), jnp.float32)
    for k, product in enumerate(products):
        hot = flat_lane == 4 * lax.rem(flat_sub, 4) + k
        message = message + jnp.where(hot, jnp.sum(product, axis=1, keepdims=True), 0.0)
    total = jnp.sum(message, axis=0, keepdims=True)

    loads[6].wait()
    for number, stage in enumerate(stages):
        slots, stage_send, stage_recv = stage_refs[3 * number : 3 * number + 3]
        size = group_size(stage, sizes)
        if size > 1:
            _, mine = partner(stage, 0)
            slots[mine] = total

            def copy_to(offset, stage=stage, slots=slots, sems=(stage_send, stage_recv)):
                where, at = partner(stage, offset)
                pltpu.make_async_remote_copy(
                    src_ref=slots.at[at], dst_ref=slots.at[at], send_sem=sems[0], recv_sem=sems[1],
                    device_id=where, device_id_type=MESH,
                ).start()

            repeat(size, copy_to)
        if number == 0:
            woven_force, woven_image = woven(0), woven(1)
            finish(2)
            woven_second = woven(2)
        if size > 1:
            where, _ = partner(stage, 1)
            others = slots.at[pl.ds(0, size - 1)]
            wait = pltpu.make_async_remote_copy(
                src_ref=others, dst_ref=others, send_sem=stage_send, recv_sem=stage_recv,
                device_id=where, device_id_type=MESH,
            )
            wait.wait_recv()
            wait.wait_send()
            total = jnp.sum(slots[...], axis=0)

    row_lane = lax.broadcasted_iota(jnp.int32, (1, 128), 1)
    live = jnp.logical_and(lax.rem(row_lane, 4) == 0, row_lane < 12)
    ff, fi, ii, si = [
        jnp.where(live, total if k == 0 else pltpu.roll(total, 128 - k, 1), 1.0) for k in range(4)
    ]
    alpha = ff / fi
    next_norm = alpha * alpha * ii - ff
    ratio = next_norm / ff
    curvature = fi - 2.0 * alpha * ii + alpha * alpha * si - ratio * next_norm / alpha
    second = next_norm / curvature
    outer = alpha + second * (1.0 + ratio)
    inner = alpha * second
    per = 2 * cx * 2 * cy
    for c in range(3):
        hot = row_lane == 4 * c
        a = jnp.sum(jnp.where(hot, outer, 0.0), axis=1, keepdims=True)
        b = jnp.sum(jnp.where(hot, inner, 0.0), axis=1, keepdims=True)
        here = slice(c * per, (c + 1) * per)
        f, q, s = woven_force[here], woven_image[here], woven_second[here]
        acc_out[c] = (a * f - b * q).reshape(2 * cx, 2 * cy, 2 * cz)
        res_out[c] = (f - a * q + b * s).reshape(2 * cx, 2 * cy, 2 * cz)

    each_z(lambda a, b, c: copy_z(a, b, c, False).wait_send())
    for phase in range(PHASES):
        each(phase, 1, lambda pair: pair[0]().wait_send())


def solution(mesh):
    sizes = tuple(mesh.shape[name] for name in AXES)

    def on_device(energy, density, region, gamma_table):
        cx, cy, cz = density.shape
        lanes = -(-(cz + LOW + HIGH + 1) // 128) * 128
        nx, ny = 2 * cx + 1, 2 * cy + 1
        out = jax.ShapeDtypeStruct((3, 2 * cx, 2 * cy, 2 * cz), jnp.float32)
        vmem = pl.BlockSpec(memory_space=pltpu.VMEM)
        hbm = pl.BlockSpec(memory_space=pltpu.HBM)
        tables = [
            padded_rows(z_matrix(cz, lanes)),
            padded_rows(plane_matrix(cx, cy)),
            weave_matrix(cz, lanes),
        ]
        assert 3 * cz % 16 == 0
        groups = -(-message_tiles(cx, cy) // PACKED)
        tile = (SUB, lanes)
        scratch = [
            pltpu.VMEM(energy.shape, jnp.float32),
            pltpu.VMEM(density.shape, jnp.float32),
            pltpu.VMEM(region.shape, jnp.int32),
            pltpu.SMEM(gamma_table.shape, jnp.float32),
            *[pltpu.VMEM(table.shape, jnp.float32) for table in tables],
            pltpu.SemaphoreType.DMA((7,)),
            pltpu.VMEM((-(-9 * cx * cy // 16) * 16, 3 * cz), jnp.float32),
            pltpu.VMEM((cx * cy, lanes), jnp.float32),
            pltpu.VMEM((-(-9 * cx * cy // 16) * 16, lanes), jnp.float32),
            pltpu.VMEM((-(-cx * cy // SUB) * SUB, lanes), jnp.float32),
            pltpu.VMEM((PHASES, ny, nx) + tile, jnp.float32),
            pltpu.VMEM((PHASES, ny, nx) + tile, jnp.float32),
            pltpu.VMEM((ny * nx * SUB, lanes), jnp.float32),
            pltpu.VMEM((2, groups) + tile, jnp.float32),
            pltpu.VMEM((PHASES, 2, ny) + tile, jnp.float32),
            pltpu.VMEM((PHASES, 2, nx) + tile, jnp.float32),
            pltpu.VMEM((PHASES, 2, 2) + tile, jnp.float32),
            pltpu.VMEM((2, 3, 3, groups) + tile, jnp.float32),
            pltpu.SemaphoreType.DMA((PHASES * 9,)),
            pltpu.SemaphoreType.DMA((PHASES * 9,)),
            pltpu.SemaphoreType.DMA((18,)),
            pltpu.SemaphoreType.DMA((18,)),
        ]
        for stage in reduction_stages(sizes):
            scratch += [
                pltpu.VMEM((group_size(stage, sizes), 1, 128), jnp.float32),
                pltpu.SemaphoreType.DMA,
                pltpu.SemaphoreType.DMA,
            ]
        return pl.pallas_call(
            functools.partial(kernel, sizes, cx, cy, cz, lanes),
            out_shape=(out, out),
            in_specs=[hbm] * 7,
            out_specs=(vmem, vmem),
            scratch_shapes=scratch,
            compiler_params=pltpu.CompilerParams(
                collective_id=0, has_side_effects=True, vmem_limit_bytes=60 * 1024 * 1024
            ),
        )(
            energy, density, region, gamma_table, *[jnp.asarray(table) for table in tables],
        )

    in_specs = (P(*AXES), P(*AXES), P(*AXES), P())
    out_specs = (P(None, *AXES), P(None, *AXES))
    return jax.shard_map(
        on_device, mesh=mesh, in_specs=in_specs, out_specs=out_specs, check_vma=False
    )
```

```python
import functools
import math

import jax
import jax.numpy as jnp
import numpy as np
from jax import lax
from jax.experimental import pallas as pl
from jax.experimental.pallas import tpu as pltpu
from jax.sharding import PartitionSpec as P

MESH = pl.DeviceIdType.MESH
AXES = ("gx", "gy", "gz")
WEIGHTS = [5.0 / 18.0, 8.0 / 18.0, 5.0 / 18.0]
SUB = 8
PHASES = 3
LOW, HIGH = 2, 1
STRIDE = 4
PACKED = 128 // STRIDE


def line_tables():
    root = math.sqrt(0.15)
    spots = [0.5 - root, 0.5, 0.5 + root]
    values = [
        [2.0 * (spot - 0.5) * (spot - 1.0), -4.0 * spot * (spot - 1.0), 2.0 * spot * (spot - 0.5)]
        for spot in spots
    ]
    slopes = [[4.0 * spot - 3.0, -8.0 * spot + 4.0, 4.0 * spot - 1.0] for spot in spots]
    return np.array(values), np.array(slopes)


def line_mass():
    values, _ = line_tables()
    return values.T @ np.diag(WEIGHTS) @ values


def line_matrix(count, table):
    out = np.zeros((2 * count + 1, 3 * count))
    for i in range(count):
        for a in range(3):
            for k in range(3):
                out[2 * i + k, 3 * i + a] += WEIGHTS[a] * table[a][k]
    return out


def plane_matrix(cx, cy):
    values, slopes = line_tables()
    vx, sx = line_matrix(cx, values), line_matrix(cx, slopes)
    vy, sy = line_matrix(cy, values), line_matrix(cy, slopes)
    nx, ny, points = 2 * cx + 1, 2 * cy + 1, 9 * cx * cy
    out = np.zeros((ny, nx, SUB, 2, -(-points // 16) * 16), np.float32)
    for c, (mx, my, part) in enumerate(((sx, vy, 0), (vx, sy, 0), (vx, vy, 1))):
        block = np.einsum("xp,yq->yxpq", mx, my).reshape(ny, nx, points)
        out[:, :, c, part, :points] = block
        out[:, :, c + 4, part, :points] = block
    return out.reshape(ny * nx * SUB, -1)


def iota(shape, dim):
    return lax.broadcasted_iota(jnp.int32, shape, dim)


def ones_where(condition):
    return jnp.where(condition, 1.0, 0.0).astype(jnp.bfloat16)


def points_to_elements(cz, lanes):
    shape = (3 * cz, lanes)
    offset = iota(shape, 0) - 3 * (iota(shape, 1) - LOW)
    return jnp.concatenate([ones_where(offset == a) for a in range(3)], axis=1)


def elements_to_nodes(cz, lanes):
    shape = (lanes, 2 * cz)
    offset = iota(shape, 1) - 2 * (iota(shape, 0) - LOW)
    return jnp.concatenate([ones_where(offset == a) for a in range(2)], axis=0)


def halves(array):
    parts = []
    rest = array
    for _ in range(3):
        piece = rest.astype(jnp.bfloat16)
        parts.append(piece)
        rest = rest - piece.astype(jnp.float32)
    return parts


def padded_rows(table):
    rows = -(-table.shape[0] // 16) * 16
    return np.pad(table, ((0, rows - table.shape[0]), (0, 0)))


def dot(a, b):
    return jnp.dot(a, b, preferred_element_type=jnp.float32)


def placed(array, table):
    count = array.shape[0]
    out = dot(jnp.concatenate(halves(array), axis=0), table)
    return out[:count] + (out[count : 2 * count] + out[2 * count :])


def by_parts(left, right, count):
    first = dot(jnp.concatenate(left, axis=0), right[0])
    second = dot(jnp.concatenate(left[:2], axis=0), right[1])
    third = dot(left[0], right[2])
    small = first[2 * count :] + second[count:] + third
    return first[:count] + (first[count : 2 * count] + second[:count] + small)


def reduction_stages(sizes):
    return [(0, 1, 2)] if math.prod(sizes) <= 64 else [(0, 1), (2,)]


def message_tiles(cx, cy):
    return (2 * cx + 1) * (2 * cy + 1) + -(-cx * cy // SUB)


def group_size(stage, sizes):
    return math.prod(sizes[axis] for axis in stage)


def axis_directions(index, size):
    if size == 1:
        return []
    if size == 2:
        return [(0, 0, 1 - 2 * index, None)]
    return [(0, 1, -1, index > 0), (1, 0, 1, index < size - 1)]


def pick(step, low, high):
    if isinstance(step, int):
        return low if step < 0 else high
    return jnp.where(step > 0, high, low)


def repeat(size, action):
    if size <= 64:
        for offset in range(1, size):
            action(offset)
    else:
        pl.loop(1, size)(action)


def under(conditions, action):
    conditions = [c for c in conditions if c is not None]
    if not conditions:
        action()
        return
    both = conditions[0]
    for c in conditions[1:]:
        both = jnp.logical_and(both, c)
    pl.when(both)(action)


def kernel(
    sizes, cx, cy, cz, lanes,
    energy_hbm, density_hbm, region_hbm, gamma_hbm, plane_hbm,
    out,
    energy, density, region, gamma, plane_mat, load_sem,
    points, fac, fac_points, dens, part, full, rows, z_part, x_buf, y_buf, xy_buf, z_buf,
    send_sem, recv_sem, z_send, z_recv, *stage_refs,
):
    loads = [
        pltpu.make_async_copy(src, dst, load_sem.at[number])
        for number, (src, dst) in enumerate((
            (energy_hbm, energy), (density_hbm, density), (region_hbm, region), (gamma_hbm, gamma),
            (plane_hbm, plane_mat),
        ))
    ]
    for load in loads:
        load.start()
    nx, ny = 2 * cx + 1, 2 * cy + 1
    nodes = nx * ny
    place = [lax.axis_index(name) for name in AXES]
    stages = reduction_stages(sizes)
    centre = (2, 2, 0, None)
    dirs = [axis_directions(place[axis], sizes[axis]) for axis in range(3)]

    def target(step_x, step_y, step_z):
        return (place[0] + step_x, place[1] + step_y, place[2] + step_z)

    def partner(stage, offset):
        mine = 0
        where = list(place)
        for axis in stage:
            mine = mine * sizes[axis] + place[axis]
        for axis in reversed(stage):
            if isinstance(offset, int):
                offset, step = divmod(offset, sizes[axis])
            else:
                offset, step = lax.div(offset, sizes[axis]), lax.rem(offset, sizes[axis])
            at = place[axis] + step
            where[axis] = jnp.where(at >= sizes[axis], at - sizes[axis], at)
        return tuple(where), mine

    for ref in (x_buf, y_buf, xy_buf, z_buf):
        ref[...] = jnp.zeros_like(ref)

    barrier = pltpu.get_barrier_semaphore()
    for stage in stages:
        size = group_size(stage, sizes)

        def greet(offset, stage=stage):
            where, _ = partner(stage, offset)
            pl.semaphore_signal(barrier, inc=1, device_id=where, device_id_type=MESH)

        repeat(size, greet)

    for load in loads[:4]:
        load.wait()
    used_points = 9 * cx * cy
    if points.shape[0] > used_points:
        spare = points.shape[0] - used_points
        points[pl.ds(used_points, spare), :] = jnp.zeros((spare, 3 * cz), jnp.float32)
        fac_points[pl.ds(used_points, spare), :] = jnp.zeros((spare, lanes), jnp.float32)
    for xp in range(3 * cx):
        points[pl.ds(xp * 3 * cy, 3 * cy), :] = energy[xp]
    gamma_elem = jnp.zeros(region.shape, jnp.float32)
    for index in range(gamma.shape[0]):
        gamma_elem = gamma_elem + jnp.where(region[...] == index, gamma[index], 0.0)
    factor = (gamma_elem - 1.0) * density[...]
    fac[...] = jnp.zeros_like(fac)
    dens[...] = jnp.zeros_like(dens)
    for i in range(cx):
        fac[pl.ds(i * cy, cy), pl.ds(LOW, cz)] = factor[i]
        dens[pl.ds(i * cy, cy), pl.ds(LOW, cz)] = density[i]
    for xp in range(3 * cx):
        for k in range(cy):
            row = fac[pl.ds((xp // 3) * cy + k, 1), :]
            fac_points[pl.ds(xp * 3 * cy + 3 * k, 3), :] = jnp.broadcast_to(row, (3, lanes))
    values, slopes = line_tables()
    spread = placed(points[...], points_to_elements(cz, lanes))
    scaled = [spread[:, a * lanes : (a + 1) * lanes] * fac_points[...] for a in range(3)]

    def node_sums(table, k):
        return sum(float(WEIGHTS[a] * table[a][k]) * scaled[a] for a in range(3))

    even = jnp.concatenate(
        [node_sums(t, 0) + pltpu.roll(node_sums(t, 2), 1, 1) for t in (values, slopes)], axis=0
    )
    odd = jnp.concatenate([node_sums(t, 1) for t in (values, slopes)], axis=0)
    loads[4].wait()
    force = by_parts(
        halves(plane_mat[...]),
        halves(jnp.concatenate([even, odd], axis=1)),
        plane_mat.shape[0],
    )[: nodes * SUB]
    sub = lax.broadcasted_iota(jnp.int32, (1, SUB, lanes), 1)
    lane = lax.broadcasted_iota(jnp.int32, (1, SUB, lanes), 2)
    is_even = sub < 4
    e_part = force[:, :lanes].reshape(nodes, SUB, lanes)
    o_part = force[:, lanes:].reshape(nodes, SUB, lanes)
    part[0] = jnp.where(is_even, e_part, o_part).reshape(ny, nx, SUB, lanes)

    top = LOW + cz
    used = jnp.logical_and(
        lax.rem(sub, 4) < 3, lane < jnp.where(is_even, top + HIGH + 1, top + HIGH)
    )
    wall_low = jnp.logical_and(place[2] == 0, jnp.logical_and(is_even, lane == LOW))
    wall_high = jnp.logical_and(
        place[2] == sizes[2] - 1, jnp.logical_and(is_even, lane == top)
    )
    keep = jnp.where(
        jnp.logical_and(used, jnp.logical_not(jnp.logical_or(wall_low, wall_high))), 1.0, 0.0
    )
    owned = jnp.where(jnp.logical_and(lane >= LOW, lane < top), 1.0, 0.0)

    flat_lane = lax.broadcasted_iota(jnp.int32, (SUB, lanes), 1)
    density_tiles = -(-cx * cy // SUB)

    def tile_of(number):
        if number < nodes:
            return part[0, number // nx, number % nx]
        return dens[pl.ds((number - nodes) * SUB, SUB), :]

    spans = ((LOW, top, HIGH + 1), (top - LOW, 0, LOW + 1))

    def pack_z():
        for side, (first, _, width) in enumerate(spans):
            for group in range(-(-(nodes + density_tiles) // PACKED)):
                tile = jnp.zeros((SUB, lanes), jnp.float32)
                for number in range(group * PACKED, min((group + 1) * PACKED, nodes + density_tiles)):
                    at = STRIDE * (number % PACKED)
                    moved = pltpu.roll(tile_of(number), (at - first) % lanes, 1)
                    hot = jnp.logical_and(flat_lane >= at, flat_lane < at + width)
                    tile = tile + jnp.where(hot, moved, 0.0)
                z_part[side, group] = tile

    def copy_z(side_z, side_x, side_y, arriving):
        (sx, tx, dx, _), (sy, ty, dy, _), (sz, tz, dz, _) = side_x, side_y, side_z
        here, there = [(c * 3 + a) * 3 + b for a, b, c in ((sx, sy, sz), (tx, ty, tz))]
        return pltpu.make_async_remote_copy(
            src_ref=z_part.at[pick(dz, 0, 1)],
            dst_ref=z_buf.at[sz, sx, sy] if arriving else z_buf.at[tz, tx, ty],
            send_sem=z_send.at[here], recv_sem=z_recv.at[here if arriving else there],
            device_id=target(dx, dy, dz), device_id_type=MESH,
        )

    def each_z(action):
        for side_z in dirs[2]:
            for side_x in dirs[0] + [centre]:
                ys = dirs[1] + [centre]
                free = [side_y for side_y in ys if side_y[3] is None]

                def run(side_z=side_z, side_x=side_x, free=free):
                    for side_y in free:
                        action(side_z, side_x, side_y)

                under([side_z[3], side_x[3]], run)
                for side_y in ys:
                    if side_y[3] is not None:
                        under(
                            [side_z[3], side_x[3], side_y[3]],
                            lambda a=side_z, b=side_x, c=side_y: action(a, b, c),
                        )

    def piece_z(side_z, sx, sy, number):
        sz, _, dz, _ = side_z
        first, width = pick(dz, 0, top), pick(dz, LOW + 1, HIGH + 1)
        if isinstance(number, int):
            group, at = divmod(number, PACKED)
        else:
            group, at = lax.div(number, PACKED), lax.rem(number, PACKED)
        shift = first - STRIDE * at
        shift = shift % lanes if isinstance(shift, int) else lax.rem(shift + lanes, lanes)
        moved = pltpu.roll(z_buf[sz, sx, sy, group], shift, 1)
        return jnp.where(jnp.logical_and(flat_lane >= first, flat_lane < first + width), moved, 0.0)

    def add_z():
        each_z(lambda a, b, c: copy_z(a, b, c, True).wait_recv())
        for number in range(nodes + density_tiles):
            if number < nodes:
                tile = full[0, number // nx, number % nx]
            else:
                tile = dens[pl.ds((number - nodes) * SUB, SUB), :]
            for side_z in dirs[2]:
                tile = tile + piece_z(side_z, 2, 2, number)
            if number < nodes:
                full[0, number // nx, number % nx] = tile
            else:
                dens[pl.ds((number - nodes) * SUB, SUB), :] = tile
        for side_x in dirs[0]:
            xf, from_x = pick(side_x[2], 0, nx - 1), pick(side_x[2], nx - 1, 0)
            for y in range(ny):
                full[0, y, xf] = full[0, y, xf] + sum(
                    piece_z(side_z, side_x[0], 2, y * nx + from_x) for side_z in dirs[2]
                )
        for side_y in dirs[1]:
            yf, from_y = pick(side_y[2], 0, ny - 1), pick(side_y[2], ny - 1, 0)
            for x in range(nx):
                full[0, yf, x] = full[0, yf, x] + sum(
                    piece_z(side_z, 2, side_y[0], from_y * nx + x) for side_z in dirs[2]
                )
            for side_x in dirs[0]:
                xf, from_x = pick(side_x[2], 0, nx - 1), pick(side_x[2], nx - 1, 0)
                full[0, yf, xf] = full[0, yf, xf] + sum(
                    piece_z(side_z, side_x[0], side_y[0], from_y * nx + from_x)
                    for side_z in dirs[2]
                )

    def copies(phase, side_x, side_y):
        (sx, tx, dx, _), (sy, ty, dy, _) = side_x, side_y
        here, there = [phase * 9 + a * 3 + b for a, b in ((sx, sy), (tx, ty))]
        xf, yf = pick(dx, 0, nx - 1), pick(dy, 0, ny - 1)
        if sy == 2:
            src = part.at[phase, :, xf]
            dst, own = x_buf.at[phase, tx], x_buf.at[phase, sx]
        elif sx == 2:
            src = part.at[phase, yf]
            dst, own = y_buf.at[phase, ty], y_buf.at[phase, sy]
        else:
            src = part.at[phase, yf, xf]
            dst, own = xy_buf.at[phase, tx, ty], xy_buf.at[phase, sx, sy]

        def make(dst_ref, slot):
            return pltpu.make_async_remote_copy(
                src_ref=src, dst_ref=dst_ref, send_sem=send_sem.at[here], recv_sem=recv_sem.at[slot],
                device_id=target(dx, dy, 0), device_id_type=MESH,
            )

        return lambda: make(dst, there), lambda: make(own, here)

    def facing(axis, step):
        chosen = []
        for direction in dirs[axis]:
            slot, at, own_step, there = direction
            if step is None:
                chosen.append(direction)
            elif isinstance(own_step, int):
                if own_step == step:
                    chosen.append(direction)
            else:
                chosen.append((slot, at, step, own_step == step))
        return chosen + [centre]

    def each(phase, step, action):
        if phase + 1 < PHASES:
            step = None
        groups = {}
        for side_x in facing(0, step):
            for side_y in facing(1, step):
                if side_x[0] == 2 and side_y[0] == 2:
                    continue
                conditions = (side_x[3], side_y[3])
                key = tuple(None if c is None else d[0] for c, d in zip(conditions, (side_x, side_y)))
                groups.setdefault(key, (conditions, []))[1].append((side_x, side_y))
        for conditions, members in groups.values():

            def run(members=members):
                for member in members:
                    action(copies(phase, *member))

            under(conditions, run)

    def start(phase):
        each(phase, 1, lambda pair: pair[0]().start())

    def finish(phase):
        each(phase, -1, lambda pair: pair[1]().wait_recv())
        full[phase] = part[phase]
        for sx, _, dx, _ in dirs[0]:
            xf = pick(dx, 0, nx - 1)
            full[phase, :, xf] = full[phase, :, xf] + x_buf[phase, sx]
        for sy, _, dy, _ in dirs[1]:
            yf = pick(dy, 0, ny - 1)
            full[phase, yf] = full[phase, yf] + y_buf[phase, sy]
            for sx, _, dx, _ in dirs[0]:
                xf = pick(dx, 0, nx - 1)
                full[phase, yf, xf] = full[phase, yf, xf] + xy_buf[phase, sx, sy]
        if phase == 0 and dirs[2]:
            add_z()
        full[phase] = full[phase] * keep.reshape(1, 1, SUB, lanes)
        for axis, last in ((0, nx - 1), (1, ny - 1)):
            for at, here in ((0, place[axis] == 0), (last, place[axis] == sizes[axis] - 1)):

                @pl.when(here)
                def _(axis=axis, at=at):
                    if axis == 0:
                        full[phase, :, at] = jnp.zeros((ny, SUB, lanes), jnp.float32)
                    else:
                        full[phase, at] = jnp.zeros((nx, SUB, lanes), jnp.float32)

    mass = [[float(v) for v in line] for line in line_mass()]

    def combine(weights, parts):
        return weights[0] * parts[0] + weights[1] * parts[1] + weights[2] * parts[2]

    on_even, on_odd, on_next = [
        jnp.where(is_even, mass[0][k], mass[1][k]).astype(jnp.float32) for k in range(3)
    ]
    even_only = jnp.where(is_even, 1.0, 0.0)

    def apply_mass(source, phase):
        lines = [full[source, y] for y in range(ny)]
        along_y = jnp.concatenate(
            [combine(mass[l], lines[2 * k : 2 * k + 3])[None] for k in range(cy) for l in range(3)],
            axis=0,
        )
        at_x = [along_y[:, x] for x in range(nx)]
        blocks = []
        for i in range(cx):
            tiles = [
                jnp.broadcast_to(dens[pl.ds(i * cy + k, 1), :], (SUB, lanes))[None]
                for k in range(cy)
                for _ in range(3)
            ]
            rho = jnp.concatenate(tiles, axis=0)
            rho_next = rho * even_only
            for j in range(3):
                t = combine(mass[j], at_x[2 * i : 2 * i + 3])
                other = pltpu.roll(t, 4, 1)
                evens, odds = jnp.where(is_even, t, other), jnp.where(is_even, other, t)
                following = pltpu.roll(evens, lanes - 1, 2)
                own = on_even * evens + on_odd * odds + on_next * following
                far = combine(mass[2], (evens, odds, following))
                blocks.append(rho * own + pltpu.roll(rho_next * far, 1, 2))
        for x in range(nx):
            i, odd_x = divmod(x, 2)
            if odd_x:
                column = blocks[3 * i + 1]
            elif x == 0:
                column = blocks[0]
            elif x == nx - 1:
                column = blocks[3 * i - 1]
            else:
                column = blocks[3 * i] + blocks[3 * i - 1]
            for y in range(ny):
                k, odd_y = divmod(y, 2)
                if odd_y:
                    value = column[3 * k + 1]
                elif y == 0:
                    value = column[0]
                elif y == ny - 1:
                    value = column[3 * k - 1]
                else:
                    value = column[3 * k] + column[3 * k - 1]
                part[phase, y, x] = value

    def woven(phase):
        rows[...] = full[phase].reshape(nodes * SUB, lanes)
        sides = []
        for first in (0, 4):
            sides.append(jnp.concatenate(
                [
                    rows[pl.ds(x * SUB + first + c, 2 * cy, stride=nx * SUB), :]
                    for c in range(3)
                    for x in range(2 * cx)
                ],
                axis=0,
            ))
        return placed(jnp.concatenate(sides, axis=1), weave)

    if sum(group_size(stage, sizes) - 1 for stage in stages):
        pl.semaphore_wait(barrier, sum(group_size(stage, sizes) - 1 for stage in stages))
    start(0)
    if dirs[2]:
        pack_z()
        each_z(lambda a, b, c: copy_z(a, b, c, False).start())
    finish(0)

    @pl.loop(0, PHASES - 1)
    def _(number):
        apply_mass(number, number + 1)

        @pl.when(number == 0)
        def _():
            start(1)
            finish(1)

    start(2)

    force_own = full[0, : ny - 1, : nx - 1].reshape(4 * cx * cy, SUB, lanes) * owned
    image_own = full[1, : ny - 1, : nx - 1].reshape(4 * cx * cy, SUB, lanes) * owned
    products = [
        jnp.sum(force_own * force_own, axis=0),
        jnp.sum(force_own * image_own, axis=0),
        jnp.sum(image_own * image_own, axis=0),
        jnp.sum((full[1] * part[2]).reshape(nodes, SUB, lanes) * owned, axis=0),
    ]
    flat_sub = lax.broadcasted_iota(jnp.int32, (SUB, 128), 0)
    message = jnp.zeros((SUB, 128), jnp.float32)
    for k, product in enumerate(products):
        hot = flat_lane == 4 * lax.rem(flat_sub, 4) + k
        message = message + jnp.where(hot, jnp.sum(product, axis=1, keepdims=True), 0.0)
    total = jnp.sum(message, axis=0, keepdims=True)

    weave = elements_to_nodes(cz, lanes)
    for number, stage in enumerate(stages):
        slots, stage_send, stage_recv = stage_refs[3 * number : 3 * number + 3]
        size = group_size(stage, sizes)
        if size > 1:
            _, mine = partner(stage, 0)
            slots[mine] = total

            def copy_to(offset, stage=stage, slots=slots, sems=(stage_send, stage_recv)):
                where, at = partner(stage, offset)
                pltpu.make_async_remote_copy(
                    src_ref=slots.at[at], dst_ref=slots.at[at], send_sem=sems[0], recv_sem=sems[1],
                    device_id=where, device_id_type=MESH,
                ).start()

            repeat(size, copy_to)
        if number == 0:
            woven_force, woven_image = woven(0), woven(1)
            finish(2)
            woven_second = woven(2)
        if size > 1:
            where, _ = partner(stage, 1)
            others = slots.at[pl.ds(0, size - 1)]
            wait = pltpu.make_async_remote_copy(
                src_ref=others, dst_ref=others, send_sem=stage_send, recv_sem=stage_recv,
                device_id=where, device_id_type=MESH,
            )
            wait.wait_recv()
            wait.wait_send()
            total = jnp.sum(slots[...], axis=0)

    row_lane = lax.broadcasted_iota(jnp.int32, (1, 128), 1)
    live = jnp.logical_and(lax.rem(row_lane, 4) == 0, row_lane < 12)
    ff, fi, ii, si = [
        jnp.where(live, total if k == 0 else pltpu.roll(total, 128 - k, 1), 1.0) for k in range(4)
    ]
    alpha = ff / fi
    next_norm = alpha * alpha * ii - ff
    ratio = next_norm / ff
    curvature = fi - 2.0 * alpha * ii + alpha * alpha * si - ratio * next_norm / alpha
    second = next_norm / curvature
    outer = alpha + second * (1.0 + ratio)
    inner = alpha * second
    per = 2 * cx * 2 * cy
    for c in range(3):
        hot = row_lane == 4 * c
        a = jnp.sum(jnp.where(hot, outer, 0.0), axis=1, keepdims=True)
        b = jnp.sum(jnp.where(hot, inner, 0.0), axis=1, keepdims=True)
        here = slice(c * per, (c + 1) * per)
        f, q, s = woven_force[here], woven_image[here], woven_second[here]
        out[0, c] = (a * f - b * q).reshape(2 * cx, 2 * cy, 2 * cz)
        out[1, c] = (f - a * q + b * s).reshape(2 * cx, 2 * cy, 2 * cz)

    each_z(lambda a, b, c: copy_z(a, b, c, False).wait_send())
    for phase in range(PHASES):
        each(phase, 1, lambda pair: pair[0]().wait_send())


def solution(mesh):
    sizes = tuple(mesh.shape[name] for name in AXES)

    def on_device(energy, density, region, gamma_table):
        cx, cy, cz = density.shape
        lanes = -(-(cz + LOW + HIGH + 1) // 128) * 128
        nx, ny = 2 * cx + 1, 2 * cy + 1
        out = jax.ShapeDtypeStruct((2, 3, 2 * cx, 2 * cy, 2 * cz), jnp.float32)
        vmem = pl.BlockSpec(memory_space=pltpu.VMEM)
        hbm = pl.BlockSpec(memory_space=pltpu.HBM)
        plane = padded_rows(plane_matrix(cx, cy))
        assert 3 * cz % 16 == 0 and lanes % 16 == 0
        groups = -(-message_tiles(cx, cy) // PACKED)
        tile = (SUB, lanes)
        scratch = [
            pltpu.VMEM(energy.shape, jnp.float32),
            pltpu.VMEM(density.shape, jnp.float32),
            pltpu.VMEM(region.shape, jnp.int32),
            pltpu.SMEM(gamma_table.shape, jnp.float32),
            pltpu.VMEM(plane.shape, jnp.float32),
            pltpu.SemaphoreType.DMA((5,)),
            pltpu.VMEM((-(-9 * cx * cy // 16) * 16, 3 * cz), jnp.float32),
            pltpu.VMEM((cx * cy, lanes), jnp.float32),
            pltpu.VMEM((-(-9 * cx * cy // 16) * 16, lanes), jnp.float32),
            pltpu.VMEM((-(-cx * cy // SUB) * SUB, lanes), jnp.float32),
            pltpu.VMEM((PHASES, ny, nx) + tile, jnp.float32),
            pltpu.VMEM((PHASES, ny, nx) + tile, jnp.float32),
            pltpu.VMEM((ny * nx * SUB, lanes), jnp.float32),
            pltpu.VMEM((2, groups) + tile, jnp.float32),
            pltpu.VMEM((PHASES, 2, ny) + tile, jnp.float32),
            pltpu.VMEM((PHASES, 2, nx) + tile, jnp.float32),
            pltpu.VMEM((PHASES, 2, 2) + tile, jnp.float32),
            pltpu.VMEM((2, 3, 3, groups) + tile, jnp.float32),
            pltpu.SemaphoreType.DMA((PHASES * 9,)),
            pltpu.SemaphoreType.DMA((PHASES * 9,)),
            pltpu.SemaphoreType.DMA((18,)),
            pltpu.SemaphoreType.DMA((18,)),
        ]
        for stage in reduction_stages(sizes):
            scratch += [
                pltpu.VMEM((group_size(stage, sizes), 1, 128), jnp.float32),
                pltpu.SemaphoreType.DMA,
                pltpu.SemaphoreType.DMA,
            ]
        both = pl.pallas_call(
            functools.partial(kernel, sizes, cx, cy, cz, lanes),
            out_shape=out,
            in_specs=[hbm] * 5,
            out_specs=vmem,
            scratch_shapes=scratch,
            compiler_params=pltpu.CompilerParams(
                collective_id=0, has_side_effects=True, vmem_limit_bytes=60 * 1024 * 1024
            ),
        )(
            energy, density, region, gamma_table, jnp.asarray(plane),
        )
        return both[0], both[1]

    in_specs = (P(*AXES), P(*AXES), P(*AXES), P())
    out_specs = (P(None, *AXES), P(None, *AXES))
    return jax.shard_map(
        on_device, mesh=mesh, in_specs=in_specs, out_specs=out_specs, check_vma=False
    )
```

```python
import functools
import math

import jax
import jax.numpy as jnp
import numpy as np
from jax import lax
from jax.experimental import pallas as pl
from jax.experimental.pallas import tpu as pltpu
from jax.sharding import PartitionSpec as P

MESH = pl.DeviceIdType.MESH
AXES = ("gx", "gy", "gz")
WEIGHTS = [5.0 / 18.0, 8.0 / 18.0, 5.0 / 18.0]
SUB = 8
PHASES = 3
LOW, HIGH = 2, 1
STRIDE = 4
PACKED = 128 // STRIDE


def line_tables():
    root = math.sqrt(0.15)
    spots = [0.5 - root, 0.5, 0.5 + root]
    values = [
        [2.0 * (spot - 0.5) * (spot - 1.0), -4.0 * spot * (spot - 1.0), 2.0 * spot * (spot - 0.5)]
        for spot in spots
    ]
    slopes = [[4.0 * spot - 3.0, -8.0 * spot + 4.0, 4.0 * spot - 1.0] for spot in spots]
    return np.array(values), np.array(slopes)


def line_mass():
    values, _ = line_tables()
    return values.T @ np.diag(WEIGHTS) @ values


def line_matrix(count, table):
    out = np.zeros((2 * count + 1, 3 * count))
    for i in range(count):
        for a in range(3):
            for k in range(3):
                out[2 * i + k, 3 * i + a] += WEIGHTS[a] * table[a][k]
    return out


def plane_matrix(cx, cy):
    values, slopes = line_tables()
    vx, sx = line_matrix(cx, values), line_matrix(cx, slopes)
    vy, sy = line_matrix(cy, values), line_matrix(cy, slopes)
    nx, ny, points = 2 * cx + 1, 2 * cy + 1, 9 * cx * cy
    out = np.zeros((ny, nx, SUB, 2, -(-points // 16) * 16), np.float32)
    for c, (mx, my, part) in enumerate(((sx, vy, 0), (vx, sy, 0), (vx, vy, 1))):
        block = np.einsum("xp,yq->yxpq", mx, my).reshape(ny, nx, points)
        out[:, :, c, part, :points] = block
        out[:, :, c + 4, part, :points] = block
    return out.reshape(ny * nx * SUB, -1)


def iota(shape, dim):
    return lax.broadcasted_iota(jnp.int32, shape, dim)


def ones_where(condition):
    return jnp.where(condition, 1.0, 0.0).astype(jnp.bfloat16)


def points_to_elements(cz, lanes):
    shape = (3 * cz, lanes)
    offset = iota(shape, 0) - 3 * (iota(shape, 1) - LOW)
    return jnp.concatenate([ones_where(offset == a) for a in range(3)], axis=1)


def elements_to_nodes(cz, lanes):
    shape = (lanes, 2 * cz)
    offset = iota(shape, 1) - 2 * (iota(shape, 0) - LOW)
    return jnp.concatenate([ones_where(offset == a) for a in range(2)], axis=0)


def halves(array):
    parts = []
    rest = array
    for _ in range(3):
        piece = rest.astype(jnp.bfloat16)
        parts.append(piece)
        rest = rest - piece.astype(jnp.float32)
    return parts


def padded_rows(table):
    rows = -(-table.shape[0] // 16) * 16
    return np.pad(table, ((0, rows - table.shape[0]), (0, 0)))


def dot(a, b):
    return jnp.dot(a, b, preferred_element_type=jnp.float32)


def placed(array, table):
    count = array.shape[0]
    out = dot(jnp.concatenate(halves(array), axis=0), table)
    return out[:count] + (out[count : 2 * count] + out[2 * count :])


def by_parts(left, right, count):
    first = dot(jnp.concatenate(left, axis=0), right[0])
    second = dot(jnp.concatenate(left[:2], axis=0), right[1])
    third = dot(left[0], right[2])
    small = first[2 * count :] + second[count:] + third
    return first[:count] + (first[count : 2 * count] + second[:count] + small)


def reduction_stages(sizes):
    return [(0, 1), (2,)]


def message_tiles(cx, cy):
    return (2 * cx + 1) * (2 * cy + 1) + -(-cx * cy // SUB)


def group_size(stage, sizes):
    return math.prod(sizes[axis] for axis in stage)


def axis_directions(index, size):
    if size == 1:
        return []
    if size == 2:
        return [(0, 0, 1 - 2 * index, None)]
    return [(0, 1, -1, index > 0), (1, 0, 1, index < size - 1)]


def pick(step, low, high):
    if isinstance(step, int):
        return low if step < 0 else high
    return jnp.where(step > 0, high, low)


def repeat(size, action):
    if size <= 64:
        for offset in range(1, size):
            action(offset)
    else:
        pl.loop(1, size)(action)


def under(conditions, action):
    conditions = [c for c in conditions if c is not None]
    if not conditions:
        action()
        return
    both = conditions[0]
    for c in conditions[1:]:
        both = jnp.logical_and(both, c)
    pl.when(both)(action)


def kernel(
    sizes, cx, cy, cz, lanes,
    energy_hbm, density_hbm, region_hbm, gamma_hbm, plane_hbm,
    out,
    energy, density, region, gamma, plane_mat, load_sem,
    points, fac, fac_points, dens, part, full, rows, z_part, x_buf, y_buf, xy_buf, z_buf,
    send_sem, recv_sem, z_send, z_recv, *stage_refs,
):
    loads = [
        pltpu.make_async_copy(src, dst, load_sem.at[number])
        for number, (src, dst) in enumerate((
            (energy_hbm, energy), (density_hbm, density), (region_hbm, region), (gamma_hbm, gamma),
            (plane_hbm, plane_mat),
        ))
    ]
    for load in loads:
        load.start()
    nx, ny = 2 * cx + 1, 2 * cy + 1
    nodes = nx * ny
    place = [lax.axis_index(name) for name in AXES]
    stages = reduction_stages(sizes)
    centre = (2, 2, 0, None)
    dirs = [axis_directions(place[axis], sizes[axis]) for axis in range(3)]

    def target(step_x, step_y, step_z):
        return (place[0] + step_x, place[1] + step_y, place[2] + step_z)

    def partner(stage, offset):
        mine = 0
        where = list(place)
        for axis in stage:
            mine = mine * sizes[axis] + place[axis]
        for axis in reversed(stage):
            if isinstance(offset, int):
                offset, step = divmod(offset, sizes[axis])
            else:
                offset, step = lax.div(offset, sizes[axis]), lax.rem(offset, sizes[axis])
            at = place[axis] + step
            where[axis] = jnp.where(at >= sizes[axis], at - sizes[axis], at)
        return tuple(where), mine

    def each_z(action):
        for side_z in dirs[2]:
            for side_x in dirs[0] + [centre]:
                ys = dirs[1] + [centre]
                free = [side_y for side_y in ys if side_y[3] is None]

                def run(side_z=side_z, side_x=side_x, free=free):
                    for side_y in free:
                        action(side_z, side_x, side_y)

                under([side_z[3], side_x[3]], run)
                for side_y in ys:
                    if side_y[3] is not None:
                        under(
                            [side_z[3], side_x[3], side_y[3]],
                            lambda a=side_z, b=side_x, c=side_y: action(a, b, c),
                        )

    for ref in (x_buf, y_buf, xy_buf, z_buf):
        ref[...] = jnp.zeros_like(ref)

    barrier = pltpu.get_barrier_semaphore()
    for stage in stages:
        size = group_size(stage, sizes)

        def greet(offset, stage=stage):
            where, _ = partner(stage, offset)
            pl.semaphore_signal(barrier, inc=1, device_id=where, device_id_type=MESH)

        repeat(size, greet)

    def greet_across(side_z, side_x, side_y):
        if side_x[0] != 2 or side_y[0] != 2:
            pl.semaphore_signal(
                barrier, inc=1, device_id=target(side_x[2], side_y[2], side_z[2]),
                device_id_type=MESH,
            )

    each_z(greet_across)

    for load in loads[:4]:
        load.wait()
    used_points = 9 * cx * cy
    if points.shape[0] > used_points:
        spare = points.shape[0] - used_points
        points[pl.ds(used_points, spare), :] = jnp.zeros((spare, 3 * cz), jnp.float32)
        fac_points[pl.ds(used_points, spare), :] = jnp.zeros((spare, lanes), jnp.float32)
    for xp in range(3 * cx):
        points[pl.ds(xp * 3 * cy, 3 * cy), :] = energy[xp]
    gamma_elem = jnp.zeros(region.shape, jnp.float32)
    for index in range(gamma.shape[0]):
        gamma_elem = gamma_elem + jnp.where(region[...] == index, gamma[index], 0.0)
    factor = (gamma_elem - 1.0) * density[...]
    fac[...] = jnp.zeros_like(fac)
    dens[...] = jnp.zeros_like(dens)
    for i in range(cx):
        fac[pl.ds(i * cy, cy), pl.ds(LOW, cz)] = factor[i]
        dens[pl.ds(i * cy, cy), pl.ds(LOW, cz)] = density[i]
    for xp in range(3 * cx):
        for k in range(cy):
            row = fac[pl.ds((xp // 3) * cy + k, 1), :]
            fac_points[pl.ds(xp * 3 * cy + 3 * k, 3), :] = jnp.broadcast_to(row, (3, lanes))
    values, slopes = line_tables()
    spread = placed(points[...], points_to_elements(cz, lanes))
    scaled = [spread[:, a * lanes : (a + 1) * lanes] * fac_points[...] for a in range(3)]

    def node_sums(table, k):
        return sum(float(WEIGHTS[a] * table[a][k]) * scaled[a] for a in range(3))

    even = jnp.concatenate(
        [node_sums(t, 0) + pltpu.roll(node_sums(t, 2), 1, 1) for t in (values, slopes)], axis=0
    )
    odd = jnp.concatenate([node_sums(t, 1) for t in (values, slopes)], axis=0)
    loads[4].wait()
    force = by_parts(
        halves(plane_mat[...]),
        halves(jnp.concatenate([even, odd], axis=1)),
        plane_mat.shape[0],
    )[: nodes * SUB]
    sub = lax.broadcasted_iota(jnp.int32, (1, SUB, lanes), 1)
    lane = lax.broadcasted_iota(jnp.int32, (1, SUB, lanes), 2)
    is_even = sub < 4
    e_part = force[:, :lanes].reshape(nodes, SUB, lanes)
    o_part = force[:, lanes:].reshape(nodes, SUB, lanes)
    part[0] = jnp.where(is_even, e_part, o_part).reshape(ny, nx, SUB, lanes)

    top = LOW + cz
    used = jnp.logical_and(
        lax.rem(sub, 4) < 3, lane < jnp.where(is_even, top + HIGH + 1, top + HIGH)
    )
    wall_low = jnp.logical_and(place[2] == 0, jnp.logical_and(is_even, lane == LOW))
    wall_high = jnp.logical_and(
        place[2] == sizes[2] - 1, jnp.logical_and(is_even, lane == top)
    )
    keep = jnp.where(
        jnp.logical_and(used, jnp.logical_not(jnp.logical_or(wall_low, wall_high))), 1.0, 0.0
    )
    owned = jnp.where(jnp.logical_and(lane >= LOW, lane < top), 1.0, 0.0)

    flat_lane = lax.broadcasted_iota(jnp.int32, (SUB, lanes), 1)
    density_tiles = -(-cx * cy // SUB)

    def tile_of(number):
        if number < nodes:
            return part[0, number // nx, number % nx]
        return dens[pl.ds((number - nodes) * SUB, SUB), :]

    spans = ((LOW, top, HIGH + 1), (top - LOW, 0, LOW + 1))

    def pack_z():
        for side, (first, _, width) in enumerate(spans):
            for group in range(-(-(nodes + density_tiles) // PACKED)):
                tile = jnp.zeros((SUB, lanes), jnp.float32)
                for number in range(group * PACKED, min((group + 1) * PACKED, nodes + density_tiles)):
                    at = STRIDE * (number % PACKED)
                    moved = pltpu.roll(tile_of(number), (at - first) % lanes, 1)
                    hot = jnp.logical_and(flat_lane >= at, flat_lane < at + width)
                    tile = tile + jnp.where(hot, moved, 0.0)
                z_part[side, group] = tile

    def copy_z(side_z, side_x, side_y, arriving):
        (sx, tx, dx, _), (sy, ty, dy, _), (sz, tz, dz, _) = side_x, side_y, side_z
        here, there = [(c * 3 + a) * 3 + b for a, b, c in ((sx, sy, sz), (tx, ty, tz))]
        return pltpu.make_async_remote_copy(
            src_ref=z_part.at[pick(dz, 0, 1)],
            dst_ref=z_buf.at[sz, sx, sy] if arriving else z_buf.at[tz, tx, ty],
            send_sem=z_send.at[here], recv_sem=z_recv.at[here if arriving else there],
            device_id=target(dx, dy, dz), device_id_type=MESH,
        )

    def piece_z(side_z, sx, sy, number):
        sz, _, dz, _ = side_z
        first, width = pick(dz, 0, top), pick(dz, LOW + 1, HIGH + 1)
        if isinstance(number, int):
            group, at = divmod(number, PACKED)
        else:
            group, at = lax.div(number, PACKED), lax.rem(number, PACKED)
        shift = first - STRIDE * at
        shift = shift % lanes if isinstance(shift, int) else lax.rem(shift + lanes, lanes)
        moved = pltpu.roll(z_buf[sz, sx, sy, group], shift, 1)
        return jnp.where(jnp.logical_and(flat_lane >= first, flat_lane < first + width), moved, 0.0)

    def add_z():
        each_z(lambda a, b, c: copy_z(a, b, c, True).wait_recv())
        for number in range(nodes + density_tiles):
            if number < nodes:
                tile = full[0, number // nx, number % nx]
            else:
                tile = dens[pl.ds((number - nodes) * SUB, SUB), :]
            for side_z in dirs[2]:
                tile = tile + piece_z(side_z, 2, 2, number)
            if number < nodes:
                full[0, number // nx, number % nx] = tile
            else:
                dens[pl.ds((number - nodes) * SUB, SUB), :] = tile
        for side_x in dirs[0]:
            xf, from_x = pick(side_x[2], 0, nx - 1), pick(side_x[2], nx - 1, 0)
            for y in range(ny):
                full[0, y, xf] = full[0, y, xf] + sum(
                    piece_z(side_z, side_x[0], 2, y * nx + from_x) for side_z in dirs[2]
                )
        for side_y in dirs[1]:
            yf, from_y = pick(side_y[2], 0, ny - 1), pick(side_y[2], ny - 1, 0)
            for x in range(nx):
                full[0, yf, x] = full[0, yf, x] + sum(
                    piece_z(side_z, 2, side_y[0], from_y * nx + x) for side_z in dirs[2]
                )
            for side_x in dirs[0]:
                xf, from_x = pick(side_x[2], 0, nx - 1), pick(side_x[2], nx - 1, 0)
                full[0, yf, xf] = full[0, yf, xf] + sum(
                    piece_z(side_z, side_x[0], side_y[0], from_y * nx + from_x)
                    for side_z in dirs[2]
                )

    def copies(phase, side_x, side_y):
        (sx, tx, dx, _), (sy, ty, dy, _) = side_x, side_y
        here, there = [phase * 9 + a * 3 + b for a, b in ((sx, sy), (tx, ty))]
        xf, yf = pick(dx, 0, nx - 1), pick(dy, 0, ny - 1)
        if sy == 2:
            src = part.at[phase, :, xf]
            dst, own = x_buf.at[phase, tx], x_buf.at[phase, sx]
        elif sx == 2:
            src = part.at[phase, yf]
            dst, own = y_buf.at[phase, ty], y_buf.at[phase, sy]
        else:
            src = part.at[phase, yf, xf]
            dst, own = xy_buf.at[phase, tx, ty], xy_buf.at[phase, sx, sy]

        def make(dst_ref, slot):
            return pltpu.make_async_remote_copy(
                src_ref=src, dst_ref=dst_ref, send_sem=send_sem.at[here], recv_sem=recv_sem.at[slot],
                device_id=target(dx, dy, 0), device_id_type=MESH,
            )

        return lambda: make(dst, there), lambda: make(own, here)

    def facing(axis, step):
        chosen = []
        for direction in dirs[axis]:
            slot, at, own_step, there = direction
            if step is None:
                chosen.append(direction)
            elif isinstance(own_step, int):
                if own_step == step:
                    chosen.append(direction)
            else:
                chosen.append((slot, at, step, own_step == step))
        return chosen + [centre]

    def each(phase, step, action):
        if phase + 1 < PHASES:
            step = None
        groups = {}
        for side_x in facing(0, step):
            for side_y in facing(1, step):
                if side_x[0] == 2 and side_y[0] == 2:
                    continue
                conditions = (side_x[3], side_y[3])
                key = tuple(None if c is None else d[0] for c, d in zip(conditions, (side_x, side_y)))
                groups.setdefault(key, (conditions, []))[1].append((side_x, side_y))
        for conditions, members in groups.values():

            def run(members=members):
                for member in members:
                    action(copies(phase, *member))

            under(conditions, run)

    def start(phase):
        each(phase, 1, lambda pair: pair[0]().start())

    def finish(phase):
        each(phase, -1, lambda pair: pair[1]().wait_recv())
        full[phase] = part[phase]
        for sx, _, dx, _ in dirs[0]:
            xf = pick(dx, 0, nx - 1)
            full[phase, :, xf] = full[phase, :, xf] + x_buf[phase, sx]
        for sy, _, dy, _ in dirs[1]:
            yf = pick(dy, 0, ny - 1)
            full[phase, yf] = full[phase, yf] + y_buf[phase, sy]
            for sx, _, dx, _ in dirs[0]:
                xf = pick(dx, 0, nx - 1)
                full[phase, yf, xf] = full[phase, yf, xf] + xy_buf[phase, sx, sy]
        if phase == 0 and dirs[2]:
            add_z()
        full[phase] = full[phase] * keep.reshape(1, 1, SUB, lanes)
        for axis, last in ((0, nx - 1), (1, ny - 1)):
            for at, here in ((0, place[axis] == 0), (last, place[axis] == sizes[axis] - 1)):

                @pl.when(here)
                def _(axis=axis, at=at):
                    if axis == 0:
                        full[phase, :, at] = jnp.zeros((ny, SUB, lanes), jnp.float32)
                    else:
                        full[phase, at] = jnp.zeros((nx, SUB, lanes), jnp.float32)

    mass = [[float(v) for v in line] for line in line_mass()]

    def combine(weights, parts):
        return weights[0] * parts[0] + weights[1] * parts[1] + weights[2] * parts[2]

    on_even, on_odd, on_next = [
        jnp.where(is_even, mass[0][k], mass[1][k]).astype(jnp.float32) for k in range(3)
    ]
    even_only = jnp.where(is_even, 1.0, 0.0)

    def apply_mass(source, phase):
        lines = [full[source, y] for y in range(ny)]
        along_y = jnp.concatenate(
            [combine(mass[l], lines[2 * k : 2 * k + 3])[None] for k in range(cy) for l in range(3)],
            axis=0,
        )
        at_x = [along_y[:, x] for x in range(nx)]
        blocks = []
        for i in range(cx):
            tiles = [
                jnp.broadcast_to(dens[pl.ds(i * cy + k, 1), :], (SUB, lanes))[None]
                for k in range(cy)
                for _ in range(3)
            ]
            rho = jnp.concatenate(tiles, axis=0)
            rho_next = rho * even_only
            for j in range(3):
                t = combine(mass[j], at_x[2 * i : 2 * i + 3])
                other = pltpu.roll(t, 4, 1)
                evens, odds = jnp.where(is_even, t, other), jnp.where(is_even, other, t)
                following = pltpu.roll(evens, lanes - 1, 2)
                own = on_even * evens + on_odd * odds + on_next * following
                far = combine(mass[2], (evens, odds, following))
                blocks.append(rho * own + pltpu.roll(rho_next * far, 1, 2))
        for x in range(nx):
            i, odd_x = divmod(x, 2)
            if odd_x:
                column = blocks[3 * i + 1]
            elif x == 0:
                column = blocks[0]
            elif x == nx - 1:
                column = blocks[3 * i - 1]
            else:
                column = blocks[3 * i] + blocks[3 * i - 1]
            for y in range(ny):
                k, odd_y = divmod(y, 2)
                if odd_y:
                    value = column[3 * k + 1]
                elif y == 0:
                    value = column[0]
                elif y == ny - 1:
                    value = column[3 * k - 1]
                else:
                    value = column[3 * k] + column[3 * k - 1]
                part[phase, y, x] = value

    def woven(phase):
        rows[...] = full[phase].reshape(nodes * SUB, lanes)
        sides = []
        for first in (0, 4):
            sides.append(jnp.concatenate(
                [
                    rows[pl.ds(x * SUB + first + c, 2 * cy, stride=nx * SUB), :]
                    for c in range(3)
                    for x in range(2 * cx)
                ],
                axis=0,
            ))
        return placed(jnp.concatenate(sides, axis=1), weave)

    def present(axis):
        there = [1 if d[3] is None else jnp.where(d[3], 1, 0) for d in dirs[axis]]
        return sum(there) if there else 0

    around = (1 + present(0)) * (1 + present(1)) - 1
    in_stages = sum(group_size(stage, sizes) - 1 for stage in stages)
    pl.semaphore_wait(barrier, in_stages + present(2) * around)
    start(0)
    if dirs[2]:
        pack_z()
        each_z(lambda a, b, c: copy_z(a, b, c, False).start())
    finish(0)

    @pl.loop(0, PHASES - 1)
    def _(number):
        apply_mass(number, number + 1)

        @pl.when(number == 0)
        def _():
            start(1)
            finish(1)

    start(2)

    force_own = full[0, : ny - 1, : nx - 1].reshape(4 * cx * cy, SUB, lanes) * owned
    image_own = full[1, : ny - 1, : nx - 1].reshape(4 * cx * cy, SUB, lanes) * owned
    products = [
        jnp.sum(force_own * force_own, axis=0),
        jnp.sum(force_own * image_own, axis=0),
        jnp.sum(image_own * image_own, axis=0),
        jnp.sum((full[1] * part[2]).reshape(nodes, SUB, lanes) * owned, axis=0),
    ]
    flat_sub = lax.broadcasted_iota(jnp.int32, (SUB, 128), 0)
    message = jnp.zeros((SUB, 128), jnp.float32)
    for k, product in enumerate(products):
        hot = flat_lane == 4 * lax.rem(flat_sub, 4) + k
        message = message + jnp.where(hot, jnp.sum(product, axis=1, keepdims=True), 0.0)
    total = jnp.sum(message, axis=0, keepdims=True)

    weave = elements_to_nodes(cz, lanes)
    for number, stage in enumerate(stages):
        slots, stage_send, stage_recv = stage_refs[3 * number : 3 * number + 3]
        size = group_size(stage, sizes)
        if size > 1:
            _, mine = partner(stage, 0)
            slots[mine] = total

            def copy_to(offset, stage=stage, slots=slots, sems=(stage_send, stage_recv)):
                where, at = partner(stage, offset)
                pltpu.make_async_remote_copy(
                    src_ref=slots.at[at], dst_ref=slots.at[at], send_sem=sems[0], recv_sem=sems[1],
                    device_id=where, device_id_type=MESH,
                ).start()

            repeat(size, copy_to)
        if number == 0:
            woven_force, woven_image = woven(0), woven(1)
        elif number == 1:
            finish(2)
            woven_second = woven(2)
        if size > 1:
            where, _ = partner(stage, 1)
            others = slots.at[pl.ds(0, size - 1)]
            wait = pltpu.make_async_remote_copy(
                src_ref=others, dst_ref=others, send_sem=stage_send, recv_sem=stage_recv,
                device_id=where, device_id_type=MESH,
            )
            wait.wait_recv()
            wait.wait_send()
            total = jnp.sum(slots[...], axis=0)

    row_lane = lax.broadcasted_iota(jnp.int32, (1, 128), 1)
    live = jnp.logical_and(lax.rem(row_lane, 4) == 0, row_lane < 12)
    ff, fi, ii, si = [
        jnp.where(live, total if k == 0 else pltpu.roll(total, 128 - k, 1), 1.0) for k in range(4)
    ]
    alpha = ff / fi
    next_norm = alpha * alpha * ii - ff
    ratio = next_norm / ff
    curvature = fi - 2.0 * alpha * ii + alpha * alpha * si - ratio * next_norm / alpha
    second = next_norm / curvature
    outer = alpha + second * (1.0 + ratio)
    inner = alpha * second
    per = 2 * cx * 2 * cy
    for c in range(3):
        hot = row_lane == 4 * c
        a = jnp.sum(jnp.where(hot, outer, 0.0), axis=1, keepdims=True)
        b = jnp.sum(jnp.where(hot, inner, 0.0), axis=1, keepdims=True)
        here = slice(c * per, (c + 1) * per)
        f, q, s = woven_force[here], woven_image[here], woven_second[here]
        out[0, c] = (a * f - b * q).reshape(2 * cx, 2 * cy, 2 * cz)
        out[1, c] = (f - a * q + b * s).reshape(2 * cx, 2 * cy, 2 * cz)

    each_z(lambda a, b, c: copy_z(a, b, c, False).wait_send())
    for phase in range(PHASES):
        each(phase, 1, lambda pair: pair[0]().wait_send())


def solution(mesh):
    sizes = tuple(mesh.shape[name] for name in AXES)

    def on_device(energy, density, region, gamma_table):
        cx, cy, cz = density.shape
        lanes = -(-(cz + LOW + HIGH + 1) // 128) * 128
        nx, ny = 2 * cx + 1, 2 * cy + 1
        out = jax.ShapeDtypeStruct((2, 3, 2 * cx, 2 * cy, 2 * cz), jnp.float32)
        vmem = pl.BlockSpec(memory_space=pltpu.VMEM)
        hbm = pl.BlockSpec(memory_space=pltpu.HBM)
        plane = padded_rows(plane_matrix(cx, cy))
        assert 3 * cz % 16 == 0 and lanes % 16 == 0
        groups = -(-message_tiles(cx, cy) // PACKED)
        tile = (SUB, lanes)
        scratch = [
            pltpu.VMEM(energy.shape, jnp.float32),
            pltpu.VMEM(density.shape, jnp.float32),
            pltpu.VMEM(region.shape, jnp.int32),
            pltpu.SMEM(gamma_table.shape, jnp.float32),
            pltpu.VMEM(plane.shape, jnp.float32),
            pltpu.SemaphoreType.DMA((5,)),
            pltpu.VMEM((-(-9 * cx * cy // 16) * 16, 3 * cz), jnp.float32),
            pltpu.VMEM((cx * cy, lanes), jnp.float32),
            pltpu.VMEM((-(-9 * cx * cy // 16) * 16, lanes), jnp.float32),
            pltpu.VMEM((-(-cx * cy // SUB) * SUB, lanes), jnp.float32),
            pltpu.VMEM((PHASES, ny, nx) + tile, jnp.float32),
            pltpu.VMEM((PHASES, ny, nx) + tile, jnp.float32),
            pltpu.VMEM((ny * nx * SUB, lanes), jnp.float32),
            pltpu.VMEM((2, groups) + tile, jnp.float32),
            pltpu.VMEM((PHASES, 2, ny) + tile, jnp.float32),
            pltpu.VMEM((PHASES, 2, nx) + tile, jnp.float32),
            pltpu.VMEM((PHASES, 2, 2) + tile, jnp.float32),
            pltpu.VMEM((2, 3, 3, groups) + tile, jnp.float32),
            pltpu.SemaphoreType.DMA((PHASES * 9,)),
            pltpu.SemaphoreType.DMA((PHASES * 9,)),
            pltpu.SemaphoreType.DMA((18,)),
            pltpu.SemaphoreType.DMA((18,)),
        ]
        for stage in reduction_stages(sizes):
            scratch += [
                pltpu.VMEM((group_size(stage, sizes), 1, 128), jnp.float32),
                pltpu.SemaphoreType.DMA,
                pltpu.SemaphoreType.DMA,
            ]
        both = pl.pallas_call(
            functools.partial(kernel, sizes, cx, cy, cz, lanes),
            out_shape=out,
            in_specs=[hbm] * 5,
            out_specs=vmem,
            scratch_shapes=scratch,
            compiler_params=pltpu.CompilerParams(
                collective_id=0, has_side_effects=True, vmem_limit_bytes=60 * 1024 * 1024
            ),
        )(
            energy, density, region, gamma_table, jnp.asarray(plane),
        )
        return both[0], both[1]

    in_specs = (P(*AXES), P(*AXES), P(*AXES), P())
    out_specs = (P(None, *AXES), P(None, *AXES))
    return jax.shard_map(
        on_device, mesh=mesh, in_specs=in_specs, out_specs=out_specs, check_vma=False
    )
```

```python
import functools
import math

import jax
import jax.numpy as jnp
import numpy as np
from jax import lax
from jax.experimental import pallas as pl
from jax.experimental.pallas import tpu as pltpu
from jax.sharding import PartitionSpec as P

MESH = pl.DeviceIdType.MESH
AXES = ("gx", "gy", "gz")
WEIGHTS = [5.0 / 18.0, 8.0 / 18.0, 5.0 / 18.0]
SUB = 8
PHASES = 3
LOW, HIGH = 2, 1
STRIDE = 4
PACKED = 128 // STRIDE


def line_tables():
    root = math.sqrt(0.15)
    spots = [0.5 - root, 0.5, 0.5 + root]
    values = [
        [2.0 * (spot - 0.5) * (spot - 1.0), -4.0 * spot * (spot - 1.0), 2.0 * spot * (spot - 0.5)]
        for spot in spots
    ]
    slopes = [[4.0 * spot - 3.0, -8.0 * spot + 4.0, 4.0 * spot - 1.0] for spot in spots]
    return np.array(values), np.array(slopes)


def line_mass():
    values, _ = line_tables()
    return values.T @ np.diag(WEIGHTS) @ values


def line_matrix(count, table):
    out = np.zeros((2 * count + 1, 3 * count))
    for i in range(count):
        for a in range(3):
            for k in range(3):
                out[2 * i + k, 3 * i + a] += WEIGHTS[a] * table[a][k]
    return out


def plane_matrix(cx, cy):
    values, slopes = line_tables()
    vx, sx = line_matrix(cx, values), line_matrix(cx, slopes)
    vy, sy = line_matrix(cy, values), line_matrix(cy, slopes)
    nx, ny, points = 2 * cx + 1, 2 * cy + 1, 9 * cx * cy
    out = np.zeros((ny, nx, SUB, 2, -(-points // 16) * 16), np.float32)
    for c, (mx, my, part) in enumerate(((sx, vy, 0), (vx, sy, 0), (vx, vy, 1))):
        block = np.einsum("xp,yq->yxpq", mx, my).reshape(ny, nx, points)
        out[:, :, c, part, :points] = block
        out[:, :, c + 4, part, :points] = block
    return out.reshape(ny * nx * SUB, -1)


def iota(shape, dim):
    return lax.broadcasted_iota(jnp.int32, shape, dim)


def ones_where(condition):
    return jnp.where(condition, 1.0, 0.0).astype(jnp.bfloat16)


def points_to_elements(cz, lanes):
    shape = (3 * cz, lanes)
    offset = iota(shape, 0) - 3 * (iota(shape, 1) - LOW)
    return jnp.concatenate([ones_where(offset == a) for a in range(3)], axis=1)


def elements_to_nodes(cz, lanes):
    shape = (lanes, 2 * cz)
    offset = iota(shape, 1) - 2 * (iota(shape, 0) - LOW)
    return jnp.concatenate([ones_where(offset == a) for a in range(2)], axis=0)


def halves(array):
    parts = []
    rest = array
    for _ in range(3):
        piece = rest.astype(jnp.bfloat16)
        parts.append(piece)
        rest = rest - piece.astype(jnp.float32)
    return parts


def padded_rows(table):
    rows = -(-table.shape[0] // 16) * 16
    return np.pad(table, ((0, rows - table.shape[0]), (0, 0)))


def dot(a, b):
    return jnp.dot(a, b, preferred_element_type=jnp.float32)


def placed(array, table):
    count = array.shape[0]
    out = dot(jnp.concatenate(halves(array), axis=0), table)
    return out[:count] + (out[count : 2 * count] + out[2 * count :])


def by_parts(left, right, count):
    first = dot(jnp.concatenate(left, axis=0), right[0])
    second = dot(jnp.concatenate(left[:2], axis=0), right[1])
    third = dot(left[0], right[2])
    small = first[2 * count :] + second[count:] + third
    return first[:count] + (first[count : 2 * count] + second[:count] + small)


def reduction_stages(sizes):
    return [(0, 1, 2)] if math.prod(sizes) <= 64 else [(0, 1), (2,)]


def message_tiles(cx, cy):
    return (2 * cx + 1) * (2 * cy + 1) + -(-cx * cy // SUB)


def group_size(stage, sizes):
    return math.prod(sizes[axis] for axis in stage)


def axis_directions(index, size):
    if size == 1:
        return []
    if size == 2:
        return [(0, 0, 1 - 2 * index, None)]
    return [(0, 1, -1, index > 0), (1, 0, 1, index < size - 1)]


def pick(step, low, high):
    if isinstance(step, int):
        return low if step < 0 else high
    return jnp.where(step > 0, high, low)


def repeat(size, action):
    if size <= 64:
        for offset in range(1, size):
            action(offset)
    else:
        pl.loop(1, size)(action)


def under(conditions, action):
    conditions = [c for c in conditions if c is not None]
    if not conditions:
        action()
        return
    both = conditions[0]
    for c in conditions[1:]:
        both = jnp.logical_and(both, c)
    pl.when(both)(action)


def kernel(
    sizes, cx, cy, cz, lanes,
    energy_hbm, density_hbm, region_hbm, gamma_hbm, plane_hbm,
    out,
    energy, density, region, gamma, plane_mat, load_sem,
    points, fac, fac_points, dens, part, full, rows, z_part, x_buf, y_buf, xy_buf, z_buf,
    send_sem, recv_sem, z_send, z_recv, *stage_refs,
):
    loads = [
        pltpu.make_async_copy(src, dst, load_sem.at[number])
        for number, (src, dst) in enumerate((
            (energy_hbm, energy), (density_hbm, density), (region_hbm, region), (gamma_hbm, gamma),
            (plane_hbm, plane_mat),
        ))
    ]
    for load in loads:
        load.start()
    nx, ny = 2 * cx + 1, 2 * cy + 1
    nodes = nx * ny
    place = [lax.axis_index(name) for name in AXES]
    stages = reduction_stages(sizes)
    centre = (2, 2, 0, None)
    dirs = [axis_directions(place[axis], sizes[axis]) for axis in range(3)]

    def target(step_x, step_y, step_z):
        return (place[0] + step_x, place[1] + step_y, place[2] + step_z)

    def partner(stage, offset):
        mine = 0
        where = list(place)
        for axis in stage:
            mine = mine * sizes[axis] + place[axis]
        for axis in reversed(stage):
            if isinstance(offset, int):
                offset, step = divmod(offset, sizes[axis])
            else:
                offset, step = lax.div(offset, sizes[axis]), lax.rem(offset, sizes[axis])
            at = place[axis] + step
            where[axis] = jnp.where(at >= sizes[axis], at - sizes[axis], at)
        return tuple(where), mine

    for ref in (x_buf, y_buf, xy_buf, z_buf):
        ref[...] = jnp.zeros_like(ref)

    barrier = pltpu.get_barrier_semaphore()
    for stage in stages:
        size = group_size(stage, sizes)

        def greet(offset, stage=stage):
            where, _ = partner(stage, offset)
            pl.semaphore_signal(barrier, inc=1, device_id=where, device_id_type=MESH)

        repeat(size, greet)

    for load in loads[:4]:
        load.wait()
    used_points = 9 * cx * cy
    if points.shape[0] > used_points:
        spare = points.shape[0] - used_points
        points[pl.ds(used_points, spare), :] = jnp.zeros((spare, 3 * cz), jnp.float32)
        fac_points[pl.ds(used_points, spare), :] = jnp.zeros((spare, lanes), jnp.float32)
    for xp in range(3 * cx):
        points[pl.ds(xp * 3 * cy, 3 * cy), :] = energy[xp]
    gamma_elem = jnp.zeros(region.shape, jnp.float32)
    for index in range(gamma.shape[0]):
        gamma_elem = gamma_elem + jnp.where(region[...] == index, gamma[index], 0.0)
    factor = (gamma_elem - 1.0) * density[...]
    fac[...] = jnp.zeros_like(fac)
    dens[...] = jnp.zeros_like(dens)
    for i in range(cx):
        fac[pl.ds(i * cy, cy), pl.ds(LOW, cz)] = factor[i]
        dens[pl.ds(i * cy, cy), pl.ds(LOW, cz)] = density[i]
    for xp in range(3 * cx):
        for k in range(cy):
            row = fac[pl.ds((xp // 3) * cy + k, 1), :]
            fac_points[pl.ds(xp * 3 * cy + 3 * k, 3), :] = jnp.broadcast_to(row, (3, lanes))
    values, slopes = line_tables()
    spread = placed(points[...], points_to_elements(cz, lanes))
    scaled = [spread[:, a * lanes : (a + 1) * lanes] * fac_points[...] for a in range(3)]

    def node_sums(table, k):
        return sum(float(WEIGHTS[a] * table[a][k]) * scaled[a] for a in range(3))

    even = jnp.concatenate(
        [node_sums(t, 0) + pltpu.roll(node_sums(t, 2), 1, 1) for t in (values, slopes)], axis=0
    )
    odd = jnp.concatenate([node_sums(t, 1) for t in (values, slopes)], axis=0)
    loads[4].wait()
    force = by_parts(
        halves(plane_mat[...]),
        halves(jnp.concatenate([even, odd], axis=1)),
        plane_mat.shape[0],
    )[: nodes * SUB]
    sub = lax.broadcasted_iota(jnp.int32, (1, SUB, lanes), 1)
    lane = lax.broadcasted_iota(jnp.int32, (1, SUB, lanes), 2)
    is_even = sub < 4
    e_part = force[:, :lanes].reshape(nodes, SUB, lanes)
    o_part = force[:, lanes:].reshape(nodes, SUB, lanes)
    part[0] = jnp.where(is_even, e_part, o_part).reshape(ny, nx, SUB, lanes)

    top = LOW + cz
    used = jnp.logical_and(
        lax.rem(sub, 4) < 3, lane < jnp.where(is_even, top + HIGH + 1, top + HIGH)
    )
    wall_low = jnp.logical_and(place[2] == 0, jnp.logical_and(is_even, lane == LOW))
    wall_high = jnp.logical_and(
        place[2] == sizes[2] - 1, jnp.logical_and(is_even, lane == top)
    )
    keep = jnp.where(
        jnp.logical_and(used, jnp.logical_not(jnp.logical_or(wall_low, wall_high))), 1.0, 0.0
    )
    owned = jnp.where(jnp.logical_and(lane >= LOW, lane < top), 1.0, 0.0)

    flat_lane = lax.broadcasted_iota(jnp.int32, (SUB, lanes), 1)
    density_tiles = -(-cx * cy // SUB)

    def tile_of(number):
        if number < nodes:
            return part[0, number // nx, number % nx]
        return dens[pl.ds((number - nodes) * SUB, SUB), :]

    spans = ((LOW, top, HIGH + 1), (top - LOW, 0, LOW + 1))

    def pack_z():
        for side, (first, _, width) in enumerate(spans):
            for group in range(-(-(nodes + density_tiles) // PACKED)):
                tile = jnp.zeros((SUB, lanes), jnp.float32)
                for number in range(group * PACKED, min((group + 1) * PACKED, nodes + density_tiles)):
                    at = STRIDE * (number % PACKED)
                    moved = pltpu.roll(tile_of(number), (at - first) % lanes, 1)
                    hot = jnp.logical_and(flat_lane >= at, flat_lane < at + width)
                    tile = tile + jnp.where(hot, moved, 0.0)
                z_part[side, group] = tile

    def copy_z(side_z, side_x, side_y, arriving):
        (sx, tx, dx, _), (sy, ty, dy, _), (sz, tz, dz, _) = side_x, side_y, side_z
        here, there = [(c * 3 + a) * 3 + b for a, b, c in ((sx, sy, sz), (tx, ty, tz))]
        return pltpu.make_async_remote_copy(
            src_ref=z_part.at[pick(dz, 0, 1)],
            dst_ref=z_buf.at[sz, sx, sy] if arriving else z_buf.at[tz, tx, ty],
            send_sem=z_send.at[here], recv_sem=z_recv.at[here if arriving else there],
            device_id=target(dx, dy, dz), device_id_type=MESH,
        )

    def each_z(action):
        for side_z in dirs[2]:
            for side_x in dirs[0] + [centre]:
                ys = dirs[1] + [centre]
                free = [side_y for side_y in ys if side_y[3] is None]

                def run(side_z=side_z, side_x=side_x, free=free):
                    for side_y in free:
                        action(side_z, side_x, side_y)

                under([side_z[3], side_x[3]], run)
                for side_y in ys:
                    if side_y[3] is not None:
                        under(
                            [side_z[3], side_x[3], side_y[3]],
                            lambda a=side_z, b=side_x, c=side_y: action(a, b, c),
                        )

    def piece_z(side_z, sx, sy, number):
        sz, _, dz, _ = side_z
        first, width = pick(dz, 0, top), pick(dz, LOW + 1, HIGH + 1)
        if isinstance(number, int):
            group, at = divmod(number, PACKED)
        else:
            group, at = lax.div(number, PACKED), lax.rem(number, PACKED)
        shift = first - STRIDE * at
        shift = shift % lanes if isinstance(shift, int) else lax.rem(shift + lanes, lanes)
        moved = pltpu.roll(z_buf[sz, sx, sy, group], shift, 1)
        return jnp.where(jnp.logical_and(flat_lane >= first, flat_lane < first + width), moved, 0.0)

    def add_z():
        each_z(lambda a, b, c: copy_z(a, b, c, True).wait_recv())
        for number in range(nodes + density_tiles):
            if number < nodes:
                tile = full[0, number // nx, number % nx]
            else:
                tile = dens[pl.ds((number - nodes) * SUB, SUB), :]
            for side_z in dirs[2]:
                tile = tile + piece_z(side_z, 2, 2, number)
            if number < nodes:
                full[0, number // nx, number % nx] = tile
            else:
                dens[pl.ds((number - nodes) * SUB, SUB), :] = tile
        for side_x in dirs[0]:
            xf, from_x = pick(side_x[2], 0, nx - 1), pick(side_x[2], nx - 1, 0)
            for y in range(ny):
                full[0, y, xf] = full[0, y, xf] + sum(
                    piece_z(side_z, side_x[0], 2, y * nx + from_x) for side_z in dirs[2]
                )
        for side_y in dirs[1]:
            yf, from_y = pick(side_y[2], 0, ny - 1), pick(side_y[2], ny - 1, 0)
            for x in range(nx):
                full[0, yf, x] = full[0, yf, x] + sum(
                    piece_z(side_z, 2, side_y[0], from_y * nx + x) for side_z in dirs[2]
                )
            for side_x in dirs[0]:
                xf, from_x = pick(side_x[2], 0, nx - 1), pick(side_x[2], nx - 1, 0)
                full[0, yf, xf] = full[0, yf, xf] + sum(
                    piece_z(side_z, side_x[0], side_y[0], from_y * nx + from_x)
                    for side_z in dirs[2]
                )

    def copies(phase, side_x, side_y):
        (sx, tx, dx, _), (sy, ty, dy, _) = side_x, side_y
        here, there = [phase * 9 + a * 3 + b for a, b in ((sx, sy), (tx, ty))]
        xf, yf = pick(dx, 0, nx - 1), pick(dy, 0, ny - 1)
        if sy == 2:
            src = part.at[phase, :, xf]
            dst, own = x_buf.at[phase, tx], x_buf.at[phase, sx]
        elif sx == 2:
            src = part.at[phase, yf]
            dst, own = y_buf.at[phase, ty], y_buf.at[phase, sy]
        else:
            src = part.at[phase, yf, xf]
            dst, own = xy_buf.at[phase, tx, ty], xy_buf.at[phase, sx, sy]

        def make(dst_ref, slot):
            return pltpu.make_async_remote_copy(
                src_ref=src, dst_ref=dst_ref, send_sem=send_sem.at[here], recv_sem=recv_sem.at[slot],
                device_id=target(dx, dy, 0), device_id_type=MESH,
            )

        return lambda: make(dst, there), lambda: make(own, here)

    def facing(axis, step):
        chosen = []
        for direction in dirs[axis]:
            slot, at, own_step, there = direction
            if step is None:
                chosen.append(direction)
            elif isinstance(own_step, int):
                if own_step == step:
                    chosen.append(direction)
            else:
                chosen.append((slot, at, step, own_step == step))
        return chosen + [centre]

    def each(phase, step, action):
        if phase + 1 < PHASES:
            step = None
        groups = {}
        for side_x in facing(0, step):
            for side_y in facing(1, step):
                if side_x[0] == 2 and side_y[0] == 2:
                    continue
                conditions = (side_x[3], side_y[3])
                key = tuple(None if c is None else d[0] for c, d in zip(conditions, (side_x, side_y)))
                groups.setdefault(key, (conditions, []))[1].append((side_x, side_y))
        for conditions, members in groups.values():

            def run(members=members):
                for member in members:
                    action(copies(phase, *member))

            under(conditions, run)

    def start(phase):
        each(phase, 1, lambda pair: pair[0]().start())

    def finish(phase):
        each(phase, -1, lambda pair: pair[1]().wait_recv())
        full[phase] = part[phase]
        for sx, _, dx, _ in dirs[0]:
            xf = pick(dx, 0, nx - 1)
            full[phase, :, xf] = full[phase, :, xf] + x_buf[phase, sx]
        for sy, _, dy, _ in dirs[1]:
            yf = pick(dy, 0, ny - 1)
            full[phase, yf] = full[phase, yf] + y_buf[phase, sy]
            for sx, _, dx, _ in dirs[0]:
                xf = pick(dx, 0, nx - 1)
                full[phase, yf, xf] = full[phase, yf, xf] + xy_buf[phase, sx, sy]
        if phase == 0 and dirs[2]:
            add_z()
        full[phase] = full[phase] * keep.reshape(1, 1, SUB, lanes)
        for axis, last in ((0, nx - 1), (1, ny - 1)):
            for at, here in ((0, place[axis] == 0), (last, place[axis] == sizes[axis] - 1)):

                @pl.when(here)
                def _(axis=axis, at=at):
                    if axis == 0:
                        full[phase, :, at] = jnp.zeros((ny, SUB, lanes), jnp.float32)
                    else:
                        full[phase, at] = jnp.zeros((nx, SUB, lanes), jnp.float32)

    mass = [[float(v) for v in line] for line in line_mass()]

    def combine(weights, parts):
        return weights[0] * parts[0] + weights[1] * parts[1] + weights[2] * parts[2]

    on_even, on_odd, on_next = [
        jnp.where(is_even, mass[0][k], mass[1][k]).astype(jnp.float32) for k in range(3)
    ]
    even_only = jnp.where(is_even, 1.0, 0.0)

    def apply_mass(source, phase):
        lines = [full[source, y] for y in range(ny)]
        along_y = jnp.concatenate(
            [combine(mass[l], lines[2 * k : 2 * k + 3])[None] for k in range(cy) for l in range(3)],
            axis=0,
        )
        at_x = [along_y[:, x] for x in range(nx)]
        blocks = []
        for i in range(cx):
            tiles = [
                jnp.broadcast_to(dens[pl.ds(i * cy + k, 1), :], (SUB, lanes))[None]
                for k in range(cy)
                for _ in range(3)
            ]
            rho = jnp.concatenate(tiles, axis=0)
            rho_next = rho * even_only
            for j in range(3):
                t = combine(mass[j], at_x[2 * i : 2 * i + 3])
                other = pltpu.roll(t, 4, 1)
                evens, odds = jnp.where(is_even, t, other), jnp.where(is_even, other, t)
                following = pltpu.roll(evens, lanes - 1, 2)
                own = on_even * evens + on_odd * odds + on_next * following
                far = combine(mass[2], (evens, odds, following))
                blocks.append(rho * own + pltpu.roll(rho_next * far, 1, 2))
        for x in range(nx):
            i, odd_x = divmod(x, 2)
            if odd_x:
                column = blocks[3 * i + 1]
            elif x == 0:
                column = blocks[0]
            elif x == nx - 1:
                column = blocks[3 * i - 1]
            else:
                column = blocks[3 * i] + blocks[3 * i - 1]
            for y in range(ny):
                k, odd_y = divmod(y, 2)
                if odd_y:
                    value = column[3 * k + 1]
                elif y == 0:
                    value = column[0]
                elif y == ny - 1:
                    value = column[3 * k - 1]
                else:
                    value = column[3 * k] + column[3 * k - 1]
                part[phase, y, x] = value

    def woven(phase):
        rows[...] = full[phase].reshape(nodes * SUB, lanes)
        sides = []
        for first in (0, 4):
            sides.append(jnp.concatenate(
                [
                    rows[pl.ds(x * SUB + first + c, 2 * cy, stride=nx * SUB), :]
                    for c in range(3)
                    for x in range(2 * cx)
                ],
                axis=0,
            ))
        return placed(jnp.concatenate(sides, axis=1), weave)

    if sum(group_size(stage, sizes) - 1 for stage in stages):
        pl.semaphore_wait(barrier, sum(group_size(stage, sizes) - 1 for stage in stages))
    start(0)
    if dirs[2]:
        pack_z()
        each_z(lambda a, b, c: copy_z(a, b, c, False).start())
    finish(0)

    @pl.loop(0, PHASES - 1)
    def _(number):
        apply_mass(number, number + 1)

        @pl.when(number == 0)
        def _():
            start(1)
            finish(1)

    start(2)

    force_own = full[0, : ny - 1, : nx - 1].reshape(4 * cx * cy, SUB, lanes) * owned
    image_own = full[1, : ny - 1, : nx - 1].reshape(4 * cx * cy, SUB, lanes) * owned
    products = [
        jnp.sum(force_own * force_own, axis=0),
        jnp.sum(force_own * image_own, axis=0),
        jnp.sum(image_own * image_own, axis=0),
        jnp.sum((full[1] * part[2]).reshape(nodes, SUB, lanes) * owned, axis=0),
    ]
    flat_sub = lax.broadcasted_iota(jnp.int32, (SUB, 128), 0)
    message = jnp.zeros((SUB, 128), jnp.float32)
    for k, product in enumerate(products):
        hot = flat_lane == 4 * lax.rem(flat_sub, 4) + k
        message = message + jnp.where(hot, jnp.sum(product, axis=1, keepdims=True), 0.0)
    total = jnp.sum(message, axis=0, keepdims=True)

    weave = elements_to_nodes(cz, lanes)
    for number, stage in enumerate(stages):
        slots, stage_send, stage_recv = stage_refs[3 * number : 3 * number + 3]
        size = group_size(stage, sizes)
        if size > 1:
            _, mine = partner(stage, 0)
            slots[mine] = total

            def copy_to(offset, stage=stage, slots=slots, sems=(stage_send, stage_recv)):
                where, at = partner(stage, offset)
                pltpu.make_async_remote_copy(
                    src_ref=slots.at[at], dst_ref=slots.at[at], send_sem=sems[0], recv_sem=sems[1],
                    device_id=where, device_id_type=MESH,
                ).start()

            repeat(size, copy_to)
        if number == 0:
            woven_force, woven_image = woven(0), woven(1)
            finish(2)
            woven_second = woven(2)
            each_z(lambda a, b, c: copy_z(a, b, c, False).wait_send())
            for phase in range(PHASES):
                each(phase, 1, lambda pair: pair[0]().wait_send())
        if size > 1:
            where, _ = partner(stage, 1)
            others = slots.at[pl.ds(0, size - 1)]
            wait = pltpu.make_async_remote_copy(
                src_ref=others, dst_ref=others, send_sem=stage_send, recv_sem=stage_recv,
                device_id=where, device_id_type=MESH,
            )
            wait.wait_recv()
            wait.wait_send()
            total = jnp.sum(slots[...], axis=0)

    row_lane = lax.broadcasted_iota(jnp.int32, (1, 128), 1)
    live = jnp.logical_and(lax.rem(row_lane, 4) == 0, row_lane < 12)
    ff, fi, ii, si = [
        jnp.where(live, total if k == 0 else pltpu.roll(total, 128 - k, 1), 1.0) for k in range(4)
    ]
    alpha = ff / fi
    next_norm = alpha * alpha * ii - ff
    ratio = next_norm / ff
    curvature = fi - 2.0 * alpha * ii + alpha * alpha * si - ratio * next_norm / alpha
    second = next_norm / curvature
    outer = alpha + second * (1.0 + ratio)
    inner = alpha * second
    per = 2 * cx * 2 * cy
    for c in range(3):
        hot = row_lane == 4 * c
        a = jnp.sum(jnp.where(hot, outer, 0.0), axis=1, keepdims=True)
        b = jnp.sum(jnp.where(hot, inner, 0.0), axis=1, keepdims=True)
        here = slice(c * per, (c + 1) * per)
        f, q, s = woven_force[here], woven_image[here], woven_second[here]
        out[0, c] = (a * f - b * q).reshape(2 * cx, 2 * cy, 2 * cz)
        out[1, c] = (f - a * q + b * s).reshape(2 * cx, 2 * cy, 2 * cz)


def solution(mesh):
    sizes = tuple(mesh.shape[name] for name in AXES)

    def on_device(energy, density, region, gamma_table):
        cx, cy, cz = density.shape
        lanes = -(-(cz + LOW + HIGH + 1) // 128) * 128
        nx, ny = 2 * cx + 1, 2 * cy + 1
        out = jax.ShapeDtypeStruct((2, 3, 2 * cx, 2 * cy, 2 * cz), jnp.float32)
        vmem = pl.BlockSpec(memory_space=pltpu.VMEM)
        hbm = pl.BlockSpec(memory_space=pltpu.HBM)
        plane = padded_rows(plane_matrix(cx, cy))
        assert 3 * cz % 16 == 0 and lanes % 16 == 0
        groups = -(-message_tiles(cx, cy) // PACKED)
        tile = (SUB, lanes)
        scratch = [
            pltpu.VMEM(energy.shape, jnp.float32),
            pltpu.VMEM(density.shape, jnp.float32),
            pltpu.VMEM(region.shape, jnp.int32),
            pltpu.SMEM(gamma_table.shape, jnp.float32),
            pltpu.VMEM(plane.shape, jnp.float32),
            pltpu.SemaphoreType.DMA((5,)),
            pltpu.VMEM((-(-9 * cx * cy // 16) * 16, 3 * cz), jnp.float32),
            pltpu.VMEM((cx * cy, lanes), jnp.float32),
            pltpu.VMEM((-(-9 * cx * cy // 16) * 16, lanes), jnp.float32),
            pltpu.VMEM((-(-cx * cy // SUB) * SUB, lanes), jnp.float32),
            pltpu.VMEM((PHASES, ny, nx) + tile, jnp.float32),
            pltpu.VMEM((PHASES, ny, nx) + tile, jnp.float32),
            pltpu.VMEM((ny * nx * SUB, lanes), jnp.float32),
            pltpu.VMEM((2, groups) + tile, jnp.float32),
            pltpu.VMEM((PHASES, 2, ny) + tile, jnp.float32),
            pltpu.VMEM((PHASES, 2, nx) + tile, jnp.float32),
            pltpu.VMEM((PHASES, 2, 2) + tile, jnp.float32),
            pltpu.VMEM((2, 3, 3, groups) + tile, jnp.float32),
            pltpu.SemaphoreType.DMA((PHASES * 9,)),
            pltpu.SemaphoreType.DMA((PHASES * 9,)),
            pltpu.SemaphoreType.DMA((18,)),
            pltpu.SemaphoreType.DMA((18,)),
        ]
        for stage in reduction_stages(sizes):
            scratch += [
                pltpu.VMEM((group_size(stage, sizes), 1, 128), jnp.float32),
                pltpu.SemaphoreType.DMA,
                pltpu.SemaphoreType.DMA,
            ]
        both = pl.pallas_call(
            functools.partial(kernel, sizes, cx, cy, cz, lanes),
            out_shape=out,
            in_specs=[hbm] * 5,
            out_specs=vmem,
            scratch_shapes=scratch,
            compiler_params=pltpu.CompilerParams(
                collective_id=0, has_side_effects=True, vmem_limit_bytes=60 * 1024 * 1024
            ),
        )(
            energy, density, region, gamma_table, jnp.asarray(plane),
        )
        return both[0], both[1]

    in_specs = (P(*AXES), P(*AXES), P(*AXES), P())
    out_specs = (P(None, *AXES), P(None, *AXES))
    return jax.shard_map(
        on_device, mesh=mesh, in_specs=in_specs, out_specs=out_specs, check_vma=False
    )
```

```python
import functools
import math

import jax
import jax.numpy as jnp
import numpy as np
from jax import lax
from jax.experimental import pallas as pl
from jax.experimental.pallas import tpu as pltpu
from jax.sharding import PartitionSpec as P

MESH = pl.DeviceIdType.MESH
AXES = ("gx", "gy", "gz")
WEIGHTS = [5.0 / 18.0, 8.0 / 18.0, 5.0 / 18.0]
SUB = 8
PHASES = 3
LOW, HIGH = 2, 1
STRIDE = 4
PACKED = 128 // STRIDE


def line_tables():
    root = math.sqrt(0.15)
    spots = [0.5 - root, 0.5, 0.5 + root]
    values = [
        [2.0 * (spot - 0.5) * (spot - 1.0), -4.0 * spot * (spot - 1.0), 2.0 * spot * (spot - 0.5)]
        for spot in spots
    ]
    slopes = [[4.0 * spot - 3.0, -8.0 * spot + 4.0, 4.0 * spot - 1.0] for spot in spots]
    return np.array(values), np.array(slopes)


def line_mass():
    values, _ = line_tables()
    return values.T @ np.diag(WEIGHTS) @ values


def line_matrix(count, table):
    out = np.zeros((2 * count + 1, 3 * count))
    for i in range(count):
        for a in range(3):
            for k in range(3):
                out[2 * i + k, 3 * i + a] += WEIGHTS[a] * table[a][k]
    return out


def plane_matrix(cx, cy):
    values, slopes = line_tables()
    vx, sx = line_matrix(cx, values), line_matrix(cx, slopes)
    vy, sy = line_matrix(cy, values), line_matrix(cy, slopes)
    nx, ny, points = 2 * cx + 1, 2 * cy + 1, 9 * cx * cy
    out = np.zeros((ny, nx, SUB, 2, -(-points // 16) * 16), np.float32)
    for c, (mx, my, part) in enumerate(((sx, vy, 0), (vx, sy, 0), (vx, vy, 1))):
        block = np.einsum("xp,yq->yxpq", mx, my).reshape(ny, nx, points)
        out[:, :, c, part, :points] = block
        out[:, :, c + 4, part, :points] = block
    return out.reshape(ny * nx * SUB, -1)


def iota(shape, dim):
    return lax.broadcasted_iota(jnp.int32, shape, dim)


def ones_where(condition):
    return jnp.where(condition, 1.0, 0.0).astype(jnp.bfloat16)


def points_to_elements(cz, lanes):
    shape = (3 * cz, lanes)
    offset = iota(shape, 0) - 3 * (iota(shape, 1) - LOW)
    return jnp.concatenate([ones_where(offset == a) for a in range(3)], axis=1)


def elements_to_nodes(cz, lanes):
    shape = (lanes, 2 * cz)
    offset = iota(shape, 1) - 2 * (iota(shape, 0) - LOW)
    return jnp.concatenate([ones_where(offset == a) for a in range(2)], axis=0)


def halves(array):
    parts = []
    rest = array
    for _ in range(3):
        piece = rest.astype(jnp.bfloat16)
        parts.append(piece)
        rest = rest - piece.astype(jnp.float32)
    return parts


def padded_rows(table):
    rows = -(-table.shape[0] // 16) * 16
    return np.pad(table, ((0, rows - table.shape[0]), (0, 0)))


def dot(a, b):
    return jnp.dot(a, b, preferred_element_type=jnp.float32)


def placed(array, table):
    count = array.shape[0]
    out = dot(jnp.concatenate(halves(array), axis=0), table)
    return out[:count] + (out[count : 2 * count] + out[2 * count :])


def by_parts(left, right, count):
    first = dot(jnp.concatenate(left, axis=0), right[0])
    second = dot(jnp.concatenate(left[:2], axis=0), right[1])
    third = dot(left[0], right[2])
    small = first[2 * count :] + second[count:] + third
    return first[:count] + (first[count : 2 * count] + second[:count] + small)


def reduction_stages(sizes):
    return [(0, 1, 2)] if math.prod(sizes) <= 64 else [(0, 1), (2,)]


def message_tiles(cx, cy):
    return (2 * cx + 1) * (2 * cy + 1) + -(-cx * cy // SUB)


def group_size(stage, sizes):
    return math.prod(sizes[axis] for axis in stage)


def axis_directions(index, size):
    if size == 1:
        return []
    if size == 2:
        return [(0, 0, 1 - 2 * index, None)]
    return [(0, 1, -1, index > 0), (1, 0, 1, index < size - 1)]


def pick(step, low, high):
    if isinstance(step, int):
        return low if step < 0 else high
    return jnp.where(step > 0, high, low)


def repeat(size, action):
    if size <= 64:
        for offset in range(1, size):
            action(offset)
    else:
        pl.loop(1, size)(action)


def under(conditions, action):
    conditions = [c for c in conditions if c is not None]
    if not conditions:
        action()
        return
    both = conditions[0]
    for c in conditions[1:]:
        both = jnp.logical_and(both, c)
    pl.when(both)(action)


def kernel(
    sizes, cx, cy, cz, lanes,
    energy_hbm, density_hbm, region_hbm, gamma_hbm, plane_hbm,
    out,
    energy, density, region, gamma, plane_mat, load_sem,
    points, fac, fac_points, dens, part, full, rows, z_part, x_buf, y_buf, xy_buf, z_buf,
    send_sem, recv_sem, z_send, z_recv, *stage_refs,
):
    loads = [
        pltpu.make_async_copy(src, dst, load_sem.at[number])
        for number, (src, dst) in enumerate((
            (energy_hbm, energy), (density_hbm, density), (region_hbm, region), (gamma_hbm, gamma),
            (plane_hbm, plane_mat),
        ))
    ]
    for load in loads:
        load.start()
    nx, ny = 2 * cx + 1, 2 * cy + 1
    nodes = nx * ny
    place = [lax.axis_index(name) for name in AXES]
    stages = reduction_stages(sizes)
    centre = (2, 2, 0, None)
    dirs = [axis_directions(place[axis], sizes[axis]) for axis in range(3)]

    def target(step_x, step_y, step_z):
        return (place[0] + step_x, place[1] + step_y, place[2] + step_z)

    def partner(stage, offset):
        mine = 0
        where = list(place)
        for axis in stage:
            mine = mine * sizes[axis] + place[axis]
        for axis in reversed(stage):
            if isinstance(offset, int):
                offset, step = divmod(offset, sizes[axis])
            else:
                offset, step = lax.div(offset, sizes[axis]), lax.rem(offset, sizes[axis])
            at = place[axis] + step
            where[axis] = jnp.where(at >= sizes[axis], at - sizes[axis], at)
        return tuple(where), mine

    for ref in (x_buf, y_buf, xy_buf, z_buf):
        ref[...] = jnp.zeros_like(ref)

    barrier = pltpu.get_barrier_semaphore()
    for stage in stages:
        size = group_size(stage, sizes)

        def greet(offset, stage=stage):
            where, _ = partner(stage, offset)
            pl.semaphore_signal(barrier, inc=1, device_id=where, device_id_type=MESH)

        repeat(size, greet)

    for load in loads[:4]:
        load.wait()
    used_points = 9 * cx * cy
    if points.shape[0] > used_points:
        spare = points.shape[0] - used_points
        points[pl.ds(used_points, spare), :] = jnp.zeros((spare, 3 * cz), jnp.float32)
        fac_points[pl.ds(used_points, spare), :] = jnp.zeros((spare, lanes), jnp.float32)
    for xp in range(3 * cx):
        points[pl.ds(xp * 3 * cy, 3 * cy), :] = energy[xp]
    gamma_elem = jnp.zeros(region.shape, jnp.float32)
    for index in range(gamma.shape[0]):
        gamma_elem = gamma_elem + jnp.where(region[...] == index, gamma[index], 0.0)
    factor = (gamma_elem - 1.0) * density[...]
    fac[...] = jnp.zeros_like(fac)
    dens[...] = jnp.zeros_like(dens)
    for i in range(cx):
        fac[pl.ds(i * cy, cy), pl.ds(LOW, cz)] = factor[i]
        dens[pl.ds(i * cy, cy), pl.ds(LOW, cz)] = density[i]
    for xp in range(3 * cx):
        for k in range(cy):
            row = fac[pl.ds((xp // 3) * cy + k, 1), :]
            fac_points[pl.ds(xp * 3 * cy + 3 * k, 3), :] = jnp.broadcast_to(row, (3, lanes))
    values, slopes = line_tables()
    spread = placed(points[...], points_to_elements(cz, lanes))
    scaled = [spread[:, a * lanes : (a + 1) * lanes] * fac_points[...] for a in range(3)]

    def node_sums(table, k):
        return sum(float(WEIGHTS[a] * table[a][k]) * scaled[a] for a in range(3))

    even = jnp.concatenate(
        [node_sums(t, 0) + pltpu.roll(node_sums(t, 2), 1, 1) for t in (values, slopes)], axis=0
    )
    odd = jnp.concatenate([node_sums(t, 1) for t in (values, slopes)], axis=0)
    loads[4].wait()
    force = by_parts(
        halves(plane_mat[...]),
        halves(jnp.concatenate([even, odd], axis=1)),
        plane_mat.shape[0],
    )[: nodes * SUB]
    sub = lax.broadcasted_iota(jnp.int32, (1, SUB, lanes), 1)
    lane = lax.broadcasted_iota(jnp.int32, (1, SUB, lanes), 2)
    is_even = sub < 4
    e_part = force[:, :lanes].reshape(nodes, SUB, lanes)
    o_part = force[:, lanes:].reshape(nodes, SUB, lanes)
    part[0] = jnp.where(is_even, e_part, o_part).reshape(ny, nx, SUB, lanes)

    top = LOW + cz
    used = jnp.logical_and(
        lax.rem(sub, 4) < 3, lane < jnp.where(is_even, top + HIGH + 1, top + HIGH)
    )
    wall_low = jnp.logical_and(place[2] == 0, jnp.logical_and(is_even, lane == LOW))
    wall_high = jnp.logical_and(
        place[2] == sizes[2] - 1, jnp.logical_and(is_even, lane == top)
    )
    keep = jnp.where(
        jnp.logical_and(used, jnp.logical_not(jnp.logical_or(wall_low, wall_high))), 1.0, 0.0
    )
    owned = jnp.where(jnp.logical_and(lane >= LOW, lane < top), 1.0, 0.0)

    flat_lane = lax.broadcasted_iota(jnp.int32, (SUB, lanes), 1)
    density_tiles = -(-cx * cy // SUB)

    def tile_of(number):
        if number < nodes:
            return part[0, number // nx, number % nx]
        return dens[pl.ds((number - nodes) * SUB, SUB), :]

    spans = ((LOW, top, HIGH + 1), (top - LOW, 0, LOW + 1))

    def pack_z():
        for side, (first, _, width) in enumerate(spans):
            for group in range(-(-(nodes + density_tiles) // PACKED)):
                tile = jnp.zeros((SUB, lanes), jnp.float32)
                for number in range(group * PACKED, min((group + 1) * PACKED, nodes + density_tiles)):
                    at = STRIDE * (number % PACKED)
                    moved = pltpu.roll(tile_of(number), (at - first) % lanes, 1)
                    hot = jnp.logical_and(flat_lane >= at, flat_lane < at + width)
                    tile = tile + jnp.where(hot, moved, 0.0)
                z_part[side, group] = tile

    def copy_z(side_z, side_x, side_y, arriving):
        (sx, tx, dx, _), (sy, ty, dy, _), (sz, tz, dz, _) = side_x, side_y, side_z
        here, there = [(c * 3 + a) * 3 + b for a, b, c in ((sx, sy, sz), (tx, ty, tz))]
        return pltpu.make_async_remote_copy(
            src_ref=z_part.at[pick(dz, 0, 1)],
            dst_ref=z_buf.at[sz, sx, sy] if arriving else z_buf.at[tz, tx, ty],
            send_sem=z_send.at[here], recv_sem=z_recv.at[here if arriving else there],
            device_id=target(dx, dy, dz), device_id_type=MESH,
        )

    def each_z(action):
        for side_z in dirs[2]:
            for side_x in dirs[0] + [centre]:
                ys = dirs[1] + [centre]
                free = [side_y for side_y in ys if side_y[3] is None]

                def run(side_z=side_z, side_x=side_x, free=free):
                    for side_y in free:
                        action(side_z, side_x, side_y)

                under([side_z[3], side_x[3]], run)
                for side_y in ys:
                    if side_y[3] is not None:
                        under(
                            [side_z[3], side_x[3], side_y[3]],
                            lambda a=side_z, b=side_x, c=side_y: action(a, b, c),
                        )

    def piece_z(side_z, sx, sy, number):
        sz, _, dz, _ = side_z
        first, width = pick(dz, 0, top), pick(dz, LOW + 1, HIGH + 1)
        if isinstance(number, int):
            group, at = divmod(number, PACKED)
        else:
            group, at = lax.div(number, PACKED), lax.rem(number, PACKED)
        shift = first - STRIDE * at
        shift = shift % lanes if isinstance(shift, int) else lax.rem(shift + lanes, lanes)
        moved = pltpu.roll(z_buf[sz, sx, sy, group], shift, 1)
        return jnp.where(jnp.logical_and(flat_lane >= first, flat_lane < first + width), moved, 0.0)

    def add_z():
        each_z(lambda a, b, c: copy_z(a, b, c, True).wait_recv())
        for number in range(nodes + density_tiles):
            if number < nodes:
                tile = full[0, number // nx, number % nx]
            else:
                tile = dens[pl.ds((number - nodes) * SUB, SUB), :]
            for side_z in dirs[2]:
                tile = tile + piece_z(side_z, 2, 2, number)
            if number < nodes:
                full[0, number // nx, number % nx] = tile
            else:
                dens[pl.ds((number - nodes) * SUB, SUB), :] = tile
        for side_x in dirs[0]:
            xf, from_x = pick(side_x[2], 0, nx - 1), pick(side_x[2], nx - 1, 0)
            for y in range(ny):
                full[0, y, xf] = full[0, y, xf] + sum(
                    piece_z(side_z, side_x[0], 2, y * nx + from_x) for side_z in dirs[2]
                )
        for side_y in dirs[1]:
            yf, from_y = pick(side_y[2], 0, ny - 1), pick(side_y[2], ny - 1, 0)
            for x in range(nx):
                full[0, yf, x] = full[0, yf, x] + sum(
                    piece_z(side_z, 2, side_y[0], from_y * nx + x) for side_z in dirs[2]
                )
            for side_x in dirs[0]:
                xf, from_x = pick(side_x[2], 0, nx - 1), pick(side_x[2], nx - 1, 0)
                full[0, yf, xf] = full[0, yf, xf] + sum(
                    piece_z(side_z, side_x[0], side_y[0], from_y * nx + from_x)
                    for side_z in dirs[2]
                )

    def copies(phase, side_x, side_y):
        (sx, tx, dx, _), (sy, ty, dy, _) = side_x, side_y
        here, there = [phase * 9 + a * 3 + b for a, b in ((sx, sy), (tx, ty))]
        xf, yf = pick(dx, 0, nx - 1), pick(dy, 0, ny - 1)
        if sy == 2:
            src = part.at[phase, :, xf]
            dst, own = x_buf.at[phase, tx], x_buf.at[phase, sx]
        elif sx == 2:
            src = part.at[phase, yf]
            dst, own = y_buf.at[phase, ty], y_buf.at[phase, sy]
        else:
            src = part.at[phase, yf, xf]
            dst, own = xy_buf.at[phase, tx, ty], xy_buf.at[phase, sx, sy]

        def make(dst_ref, slot):
            return pltpu.make_async_remote_copy(
                src_ref=src, dst_ref=dst_ref, send_sem=send_sem.at[here], recv_sem=recv_sem.at[slot],
                device_id=target(dx, dy, 0), device_id_type=MESH,
            )

        return lambda: make(dst, there), lambda: make(own, here)

    def facing(axis, step):
        chosen = []
        for direction in dirs[axis]:
            slot, at, own_step, there = direction
            if step is None:
                chosen.append(direction)
            elif isinstance(own_step, int):
                if own_step == step:
                    chosen.append(direction)
            else:
                chosen.append((slot, at, step, own_step == step))
        return chosen + [centre]

    def each(phase, step, action):
        if phase + 1 < PHASES:
            step = None
        groups = {}
        for side_x in facing(0, step):
            for side_y in facing(1, step):
                if side_x[0] == 2 and side_y[0] == 2:
                    continue
                conditions = (side_x[3], side_y[3])
                key = tuple(None if c is None else d[0] for c, d in zip(conditions, (side_x, side_y)))
                groups.setdefault(key, (conditions, []))[1].append((side_x, side_y))
        for conditions, members in groups.values():

            def run(members=members):
                for member in members:
                    action(copies(phase, *member))

            under(conditions, run)

    def start(phase):
        each(phase, 1, lambda pair: pair[0]().start())

    def finish(phase):
        each(phase, -1, lambda pair: pair[1]().wait_recv())
        full[phase] = part[phase]
        for sx, _, dx, _ in dirs[0]:
            xf = pick(dx, 0, nx - 1)
            full[phase, :, xf] = full[phase, :, xf] + x_buf[phase, sx]
        for sy, _, dy, _ in dirs[1]:
            yf = pick(dy, 0, ny - 1)
            full[phase, yf] = full[phase, yf] + y_buf[phase, sy]
            for sx, _, dx, _ in dirs[0]:
                xf = pick(dx, 0, nx - 1)
                full[phase, yf, xf] = full[phase, yf, xf] + xy_buf[phase, sx, sy]
        if phase == 0 and dirs[2]:
            add_z()
        full[phase] = full[phase] * keep.reshape(1, 1, SUB, lanes)
        for axis, last in ((0, nx - 1), (1, ny - 1)):
            for at, here in ((0, place[axis] == 0), (last, place[axis] == sizes[axis] - 1)):

                @pl.when(here)
                def _(axis=axis, at=at):
                    if axis == 0:
                        full[phase, :, at] = jnp.zeros((ny, SUB, lanes), jnp.float32)
                    else:
                        full[phase, at] = jnp.zeros((nx, SUB, lanes), jnp.float32)

    mass = [[float(v) for v in line] for line in line_mass()]

    def combine(weights, parts):
        return weights[0] * parts[0] + weights[1] * parts[1] + weights[2] * parts[2]

    on_even, on_odd, on_next = [
        jnp.where(is_even, mass[0][k], mass[1][k]).astype(jnp.float32) for k in range(3)
    ]
    even_only = jnp.where(is_even, 1.0, 0.0)

    def apply_mass(source, phase):
        lines = [full[source, y] for y in range(ny)]
        along_y = jnp.concatenate(
            [combine(mass[l], lines[2 * k : 2 * k + 3])[None] for k in range(cy) for l in range(3)],
            axis=0,
        )
        at_x = [along_y[:, x] for x in range(nx)]
        blocks = []
        for i in range(cx):
            tiles = [
                jnp.broadcast_to(dens[pl.ds(i * cy + k, 1), :], (SUB, lanes))[None]
                for k in range(cy)
                for _ in range(3)
            ]
            rho = jnp.concatenate(tiles, axis=0)
            rho_next = rho * even_only
            for j in range(3):
                t = combine(mass[j], at_x[2 * i : 2 * i + 3])
                other = pltpu.roll(t, 4, 1)
                evens, odds = jnp.where(is_even, t, other), jnp.where(is_even, other, t)
                following = pltpu.roll(evens, lanes - 1, 2)
                own = on_even * evens + on_odd * odds + on_next * following
                far = combine(mass[2], (evens, odds, following))
                blocks.append(rho * own + pltpu.roll(rho_next * far, 1, 2))
        for x in range(nx):
            i, odd_x = divmod(x, 2)
            if odd_x:
                column = blocks[3 * i + 1]
            elif x == 0:
                column = blocks[0]
            elif x == nx - 1:
                column = blocks[3 * i - 1]
            else:
                column = blocks[3 * i] + blocks[3 * i - 1]
            for y in range(ny):
                k, odd_y = divmod(y, 2)
                if odd_y:
                    value = column[3 * k + 1]
                elif y == 0:
                    value = column[0]
                elif y == ny - 1:
                    value = column[3 * k - 1]
                else:
                    value = column[3 * k] + column[3 * k - 1]
                part[phase, y, x] = value

    def woven(phase):
        rows[...] = full[phase].reshape(nodes * SUB, lanes)
        sides = []
        for first in (0, 4):
            sides.append(jnp.concatenate(
                [
                    rows[pl.ds(x * SUB + first + c, 2 * cy, stride=nx * SUB), :]
                    for c in range(3)
                    for x in range(2 * cx)
                ],
                axis=0,
            ))
        return placed(jnp.concatenate(sides, axis=1), weave)

    if sum(group_size(stage, sizes) - 1 for stage in stages):
        pl.semaphore_wait(barrier, sum(group_size(stage, sizes) - 1 for stage in stages))
    if dirs[2]:
        pack_z()
        each_z(lambda a, b, c: copy_z(a, b, c, False).start())
    start(0)
    finish(0)

    @pl.loop(0, PHASES - 1)
    def _(number):
        apply_mass(number, number + 1)

        @pl.when(number == 0)
        def _():
            start(1)
            finish(1)

    start(2)

    force_own = full[0, : ny - 1, : nx - 1].reshape(4 * cx * cy, SUB, lanes) * owned
    image_own = full[1, : ny - 1, : nx - 1].reshape(4 * cx * cy, SUB, lanes) * owned
    products = [
        jnp.sum(force_own * force_own, axis=0),
        jnp.sum(force_own * image_own, axis=0),
        jnp.sum(image_own * image_own, axis=0),
        jnp.sum((full[1] * part[2]).reshape(nodes, SUB, lanes) * owned, axis=0),
    ]
    flat_sub = lax.broadcasted_iota(jnp.int32, (SUB, 128), 0)
    message = jnp.zeros((SUB, 128), jnp.float32)
    for k, product in enumerate(products):
        hot = flat_lane == 4 * lax.rem(flat_sub, 4) + k
        message = message + jnp.where(hot, jnp.sum(product, axis=1, keepdims=True), 0.0)
    total = jnp.sum(message, axis=0, keepdims=True)

    weave = elements_to_nodes(cz, lanes)
    for number, stage in enumerate(stages):
        slots, stage_send, stage_recv = stage_refs[3 * number : 3 * number + 3]
        size = group_size(stage, sizes)
        if size > 1:
            _, mine = partner(stage, 0)
            slots[mine] = total

            def copy_to(offset, stage=stage, slots=slots, sems=(stage_send, stage_recv)):
                where, at = partner(stage, offset)
                pltpu.make_async_remote_copy(
                    src_ref=slots.at[at], dst_ref=slots.at[at], send_sem=sems[0], recv_sem=sems[1],
                    device_id=where, device_id_type=MESH,
                ).start()

            repeat(size, copy_to)
        if number == 0:
            woven_force, woven_image = woven(0), woven(1)
            finish(2)
            woven_second = woven(2)
            each_z(lambda a, b, c: copy_z(a, b, c, False).wait_send())
            for phase in range(PHASES):
                each(phase, 1, lambda pair: pair[0]().wait_send())
        if size > 1:
            where, _ = partner(stage, 1)
            others = slots.at[pl.ds(0, size - 1)]
            wait = pltpu.make_async_remote_copy(
                src_ref=others, dst_ref=others, send_sem=stage_send, recv_sem=stage_recv,
                device_id=where, device_id_type=MESH,
            )
            wait.wait_recv()
            wait.wait_send()
            total = jnp.sum(slots[...], axis=0)

    row_lane = lax.broadcasted_iota(jnp.int32, (1, 128), 1)
    live = jnp.logical_and(lax.rem(row_lane, 4) == 0, row_lane < 12)
    ff, fi, ii, si = [
        jnp.where(live, total if k == 0 else pltpu.roll(total, 128 - k, 1), 1.0) for k in range(4)
    ]
    alpha = ff / fi
    next_norm = alpha * alpha * ii - ff
    ratio = next_norm / ff
    curvature = fi - 2.0 * alpha * ii + alpha * alpha * si - ratio * next_norm / alpha
    second = next_norm / curvature
    outer = alpha + second * (1.0 + ratio)
    inner = alpha * second
    per = 2 * cx * 2 * cy
    for c in range(3):
        hot = row_lane == 4 * c
        a = jnp.sum(jnp.where(hot, outer, 0.0), axis=1, keepdims=True)
        b = jnp.sum(jnp.where(hot, inner, 0.0), axis=1, keepdims=True)
        here = slice(c * per, (c + 1) * per)
        f, q, s = woven_force[here], woven_image[here], woven_second[here]
        out[0, c] = (a * f - b * q).reshape(2 * cx, 2 * cy, 2 * cz)
        out[1, c] = (f - a * q + b * s).reshape(2 * cx, 2 * cy, 2 * cz)


def solution(mesh):
    sizes = tuple(mesh.shape[name] for name in AXES)

    def on_device(energy, density, region, gamma_table):
        cx, cy, cz = density.shape
        lanes = -(-(cz + LOW + HIGH + 1) // 128) * 128
        nx, ny = 2 * cx + 1, 2 * cy + 1
        out = jax.ShapeDtypeStruct((2, 3, 2 * cx, 2 * cy, 2 * cz), jnp.float32)
        vmem = pl.BlockSpec(memory_space=pltpu.VMEM)
        hbm = pl.BlockSpec(memory_space=pltpu.HBM)
        plane = padded_rows(plane_matrix(cx, cy))
        assert 3 * cz % 16 == 0 and lanes % 16 == 0
        groups = -(-message_tiles(cx, cy) // PACKED)
        tile = (SUB, lanes)
        scratch = [
            pltpu.VMEM(energy.shape, jnp.float32),
            pltpu.VMEM(density.shape, jnp.float32),
            pltpu.VMEM(region.shape, jnp.int32),
            pltpu.SMEM(gamma_table.shape, jnp.float32),
            pltpu.VMEM(plane.shape, jnp.float32),
            pltpu.SemaphoreType.DMA((5,)),
            pltpu.VMEM((-(-9 * cx * cy // 16) * 16, 3 * cz), jnp.float32),
            pltpu.VMEM((cx * cy, lanes), jnp.float32),
            pltpu.VMEM((-(-9 * cx * cy // 16) * 16, lanes), jnp.float32),
            pltpu.VMEM((-(-cx * cy // SUB) * SUB, lanes), jnp.float32),
            pltpu.VMEM((PHASES, ny, nx) + tile, jnp.float32),
            pltpu.VMEM((PHASES, ny, nx) + tile, jnp.float32),
            pltpu.VMEM((ny * nx * SUB, lanes), jnp.float32),
            pltpu.VMEM((2, groups) + tile, jnp.float32),
            pltpu.VMEM((PHASES, 2, ny) + tile, jnp.float32),
            pltpu.VMEM((PHASES, 2, nx) + tile, jnp.float32),
            pltpu.VMEM((PHASES, 2, 2) + tile, jnp.float32),
            pltpu.VMEM((2, 3, 3, groups) + tile, jnp.float32),
            pltpu.SemaphoreType.DMA((PHASES * 9,)),
            pltpu.SemaphoreType.DMA((PHASES * 9,)),
            pltpu.SemaphoreType.DMA((18,)),
            pltpu.SemaphoreType.DMA((18,)),
        ]
        for stage in reduction_stages(sizes):
            scratch += [
                pltpu.VMEM((group_size(stage, sizes), 1, 128), jnp.float32),
                pltpu.SemaphoreType.DMA,
                pltpu.SemaphoreType.DMA,
            ]
        both = pl.pallas_call(
            functools.partial(kernel, sizes, cx, cy, cz, lanes),
            out_shape=out,
            in_specs=[hbm] * 5,
            out_specs=vmem,
            scratch_shapes=scratch,
            compiler_params=pltpu.CompilerParams(
                collective_id=0, has_side_effects=True, vmem_limit_bytes=60 * 1024 * 1024
            ),
        )(
            energy, density, region, gamma_table, jnp.asarray(plane),
        )
        return both[0], both[1]

    in_specs = (P(*AXES), P(*AXES), P(*AXES), P())
    out_specs = (P(None, *AXES), P(None, *AXES))
    return jax.shard_map(
        on_device, mesh=mesh, in_specs=in_specs, out_specs=out_specs, check_vma=False
    )
```
